256 devices in a mesh: section: 4 (over x_lo, core), expert: 16 (over z, x_hi), tensor: 4 (over y).
Axes of the slice: x: 4 (x_hi: 2, x_lo: 2; x = x_hi * 2 + x_lo), y: 4, z: 8, core: 2. Of those that a mesh axis runs over, the one named last changes fastest.
Arguments:
- tokens: bfloat16 [4, 2048, 4096], P('section', 'expert', 'tensor'), may hold values from -6 to 6
- expert_ids: int32 [4, 2048, 8], P('section', 'expert'), may hold values from 0 to 15, all different within a row; in each aligned block of 128 rows (0 to 127, 128 to 255, ..., all dimensions but the last counted through in order) at most 72 rows name the same one
- gate_values: float32 [4, 2048, 8], P('section', 'expert'), may hold values from 0.05 to 0.5
- w_gate: bfloat16 [4, 16, 4096, 1536], P('section', 'expert', None, 'tensor'), may hold values from -0.09375 to 0.09375
- w_up: bfloat16 [4, 16, 4096, 1536], P('section', 'expert', None, 'tensor'), may hold values from -0.09375 to 0.09375
- w_down: bfloat16 [4, 16, 1536, 4096], P('section', 'expert', 'tensor'), may hold values from -0.15625 to 0.15625
Outputs:
- next_input: bfloat16 [4, 2048, 4096], P('section', 'expert', 'tensor')
The draws below stay inside these ranges and needn't reach their ends.
Inputs may be any that keep to these rules, and one draw needn't show every extreme that they name: `expert_ids`: each row names 8 different experts. Among the rows of one index of the expert axis in one section, no expert is named more than 72 times, a bound that some block reaches.
All inputs are finite; a program needn't handle non-finite values.
Results may differ from the reference program's by a relative error of at most 0.0049.
Values may be sent and summed in bfloat16 or wider, within the bound.
A program may use at most 128 MiB of HBM per device.

```python
import math
import jax
import jax.numpy as jnp
import numpy as np
from jax import lax

D = 4096
FF = 1536
TOP = 8
TOK_DEV = 128
EXPERTS = 16
CAP = 72
TOKENS = 2048
N_SECTION = 4
N_EXPERT = 16


def levels(key, dims, pieces, smallest, largest):
    level = 1.0
    for dim, shards_of in pieces:
        steps = jax.random.uniform(jax.random.fold_in(jax.random.fold_in(key, 6), dim), (shards_of,), jnp.float32, smallest / len(pieces), largest / len(pieces))
        level = level * jnp.repeat(jnp.exp(steps), dims[dim] // shards_of).reshape((-1,) + (1,) * (len(dims) - 1 - dim))
    return level


def assign_block(own_key, own, number, rows, count, top, reach, slope):
    ranking = jax.random.permutation(own_key, count)
    heavy_load, usual = shares(count, rows * top, reach, slope, True), shares(count, rows * top, reach, slope, False)
    places = jnp.arange(count)

    def named(lengths, turn):
        used = int((lengths > 0).sum())
        fixed = max(1, used // 4)
        passed = fixed + (places - fixed + turn * (used - fixed)) % max(1, count - fixed)
        return jnp.zeros((count,), jnp.int32).at[ranking[jnp.where(places < fixed, places, passed)]].set(jnp.asarray(lengths, jnp.int32))

    lengths = jnp.where(number % 4 == 0, named(heavy_load, number // 4), named(usual, number - number // 4 - 1))
    mixed = jax.random.permutation(jax.random.fold_in(own, 3), count)
    donor, taker = mixed[0:count // 2 * 2:2], mixed[1:count // 2 * 2:2]
    margin = jnp.minimum(lengths[donor] - 1, reach - lengths[taker]) // 2
    margin = jnp.where((donor == ranking[0]) | (taker == ranking[0]) | (lengths[taker] == 0), 0, jnp.maximum(margin, 0))
    passed = jax.random.randint(jax.random.fold_in(own, 4), (count // 2,), 0, 1 << 20) % (margin + 1)
    lengths = lengths.at[donor].add(-passed).at[taker].add(passed)
    labels = jnp.searchsorted(jnp.cumsum(lengths), jnp.arange(rows * top), side="right").astype(jnp.int32)
    listing = labels.reshape(top, rows).T
    listing = listing[jax.random.permutation(jax.random.fold_in(own, 1), rows)]
    turn = jax.random.randint(jax.random.fold_in(own, 2), (rows, 1), 0, top)
    return jnp.take_along_axis(listing, (jnp.arange(top)[None, :] + turn) % top, axis=1)


def shares(count, total, limit, slope, full):
    weights = [(1 << 20) // math.isqrt(grade ** slope) + 1 for grade in range(1, count + 1)]
    largest = limit if full else min(limit, max(-(-total // count), total * weights[0] // sum(weights)))
    least = 1 if total - largest >= count - 1 else 0
    holding, spare = [largest] + [least] * (count - 1), total - largest - least * (count - 1)
    while spare > 0:
        movable = [i for i in range(1, count) if holding[i] < largest] or [i for i in range(1, count) if holding[i] < limit]
        pool, left = sum([weights[i] for i in movable]), spare
        for i in movable:
            extra = min(limit - holding[i], max(1, left * weights[i] // pool), spare)
            holding[i] = holding[i] + extra
            spare = spare - extra
    return np.array(holding)


def normal_values(stream_key, extent, deviation, limit, shards=(), kind=jnp.bfloat16):
    entries = jax.random.normal(stream_key, extent, jnp.float32) * deviation
    if len(shards) > 0:
        entries = levels(stream_key, extent, shards, -0.22, 0.18) * entries
    return jnp.clip(entries, min=-limit, max=limit).astype(kind)


def setup_inputs(seed: int = 0) -> dict:
    key_list = jax.random.split(jax.random.key(seed), 7)
    tokens = normal_values(key_list[0], (N_SECTION, TOKENS, D), 1.0, 6.0, ((0, 4), (1, 16), (2, 4)))
    expert_ids_keys = jax.random.split(jax.random.fold_in(key_list[1], 1), N_SECTION * TOKENS // TOK_DEV)
    expert_ids_turns = jax.random.permutation(jax.random.fold_in(key_list[1], 3), N_SECTION * TOKENS // TOK_DEV)
    expert_ids = jax.vmap(lambda own, number: assign_block(jax.random.fold_in(key_list[1], 2), own, number, TOK_DEV, EXPERTS, TOP, CAP, 1))(expert_ids_keys, expert_ids_turns).reshape((N_SECTION, TOKENS, TOP))
    gate_values = jnp.clip(jnp.exp(math.log(0.5) - 2.3025851 * jax.random.uniform(key_list[2], (N_SECTION, TOKENS, TOP), jnp.float32) ** levels(key_list[2], (N_SECTION, TOKENS, TOP), ((0, 4), (1, 16)), -0.2, 0.2)), 0.05, 0.5)
    w_gate = normal_values(key_list[3], (N_SECTION, EXPERTS, D, FF), D ** -0.5, 0.09375, ((0, 4), (1, 16), (3, 4)))
    w_up = normal_values(key_list[4], (N_SECTION, EXPERTS, D, FF), D ** -0.5, 0.09375, ((0, 4), (1, 16), (3, 4)))
    w_down = normal_values(key_list[5], (N_SECTION, EXPERTS, FF, D), FF ** -0.5, 0.15625, ((0, 4), (1, 16), (2, 4)))
    return {"tokens": tokens, "expert_ids": expert_ids, "gate_values": gate_values, "w_gate": w_gate, "w_up": w_up, "w_down": w_down}


def expert_slots(pair_experts, expert_index, slot_count):
    chosen = (pair_experts == expert_index).astype(jnp.int32)
    position = jnp.cumsum(chosen) - 1
    target = jnp.where(chosen > 0, position, slot_count).astype(jnp.int32)
    pair_index = jnp.arange(pair_experts.shape[0], dtype=jnp.int32)
    slot_pair = jnp.zeros((slot_count,), jnp.int32).at[target].set(pair_index, mode="drop")
    is_valid = jnp.zeros((slot_count,), jnp.int32).at[target].set(1, mode="drop")
    return slot_pair, is_valid


def reference(tokens, expert_ids, gate_values, w_gate, w_up, w_down):
    section_outputs = []
    for section in range(N_SECTION):
        pair_experts = expert_ids[section].reshape(-1).astype(jnp.int32)
        pair_gates = gate_values[section].reshape(-1)
        section_rows = tokens[section]

        def add_expert(running, expert_items):
            expert_index, gate_w, up_w, down_w = expert_items
            slot_pair, is_valid = expert_slots(pair_experts, expert_index, N_EXPERT * CAP)
            slot_token = (slot_pair // TOP).astype(jnp.int32)
            slot_rows = section_rows[slot_token]
            gate_act = jnp.dot(slot_rows, gate_w, preferred_element_type=jnp.float32)
            up_act = jnp.dot(slot_rows, up_w, preferred_element_type=jnp.float32)
            hidden = (jax.nn.silu(gate_act) * up_act).astype(jnp.bfloat16)
            expert_out = jnp.dot(hidden, down_w, preferred_element_type=jnp.float32)
            weight = pair_gates[slot_pair] * is_valid.astype(pair_gates.dtype)
            return running.at[slot_token].add(expert_out * weight[:, None]), None

        start = jnp.zeros((TOKENS, D), jnp.float32)
        running, _ = lax.scan(add_expert, start, (jnp.arange(EXPERTS, dtype=jnp.int32), w_gate[section], w_up[section], w_down[section]))
        section_outputs.append(running.astype(jnp.bfloat16))
    combined = jnp.stack(section_outputs)
    return jnp.roll(combined, 1, axis=0)
```

```python
import functools

import jax
import jax.numpy as jnp
from jax import lax
from jax.experimental import pallas as pl
from jax.experimental.pallas import tpu as pltpu
from jax.sharding import PartitionSpec as P

CAP = 72
PAD = 80
NAMES = 16
BF16 = jnp.bfloat16
F32 = jnp.float32


def iota(shape, dim):
    return lax.broadcasted_iota(jnp.int32, shape, dim)


def dot(a, b):
    return jnp.dot(a, b, preferred_element_type=F32)


def moe_kernel(
    nsec, nz, ny,
    tok_ref, ids_ref, gate_ref, wg_hbm, wu_hbm, wd_hbm, out_ref,
    wg, wu, wd, table, slot_t, tok2, xs, xg, slot_out, slot_in, xb, px, pr, x1, hidden,
    s1, r1, s2, r2, s3, r3, ret, back, mix, acc,
    w_sem, meta_send, meta_recv, tok_send, tok_recv, z_send, z_recv, slot_send, slot_recv,
    b1_send, b1_recv, b2_send, b2_recv, ring_send, ring_recv, tail_send, tail_recv, x_send, x_recv,
    g1_send, g1_recv, g2_send, g2_recv, r1_send, r1_recv, r2_send, r2_recv, r3_send, r3_recv,
    back_send, back_recv,
):
    sec, e, t = lax.axis_index("section"), lax.axis_index("expert"), lax.axis_index("tensor")
    z, xh = lax.div(e, 2), lax.rem(e, 2)
    rows, quarter = tok_ref.shape
    half = quarter // 2
    late = xg.shape[3]
    pair = 2 * CAP
    right, left, opposite = lax.rem(t + 1, ny), lax.rem(t + ny - 1, ny), lax.rem(t + 2, ny)
    after, before = lax.rem(sec + 1, nsec), lax.rem(sec + nsec - 1, nsec)

    def away(k):
        return lax.rem(lax.div(k + 1, 2) * (2 * lax.rem(k, 2) - 1) + nz, nz)

    def z_to(k):
        return lax.rem(z + away(k), nz)

    def z_from(k):
        return lax.rem(z - away(k) + nz, nz)

    loads = [
        pltpu.make_async_copy(wg_hbm, wg, w_sem.at[0]),
        pltpu.make_async_copy(wu_hbm, wu, w_sem.at[1]),
    ] + [
        pltpu.make_async_copy(wd_hbm.at[:, pl.ds(q * quarter, quarter)], wd.at[q], w_sem.at[2 + q])
        for q in range(ny)
    ]
    for load in loads:
        load.start()

    named = iota((NAMES, rows), 0)
    own = jnp.zeros((NAMES, rows), F32)
    for k in range(ids_ref.shape[0]):
        own = own + jnp.where(ids_ref[k : k + 1, :] == named, gate_ref[k : k + 1, :], 0.0)
    table[xh] = own

    barrier = pltpu.get_barrier_semaphore()

    def greet(device):
        pl.semaphore_signal(barrier, inc=1, device_id=device, device_id_type=pl.DeviceIdType.MESH)

    partner = (sec, z * 2 + 1 - xh, t)
    to_right, to_left = (sec, e, right), (sec, e, left)
    greet(to_right)
    greet(to_left)
    greet(partner)
    for k in range(1, nz):
        greet((sec, z_from(k) * 2 + xh, t))
    for other in range(2 * nz):
        greet((before, other, t))
    pl.semaphore_wait(barrier, (nz - 1) + 3 + 2 * nz)

    def push(src, dst, send, recv, device):
        return pltpu.make_async_remote_copy(
            src_ref=src, dst_ref=dst, send_sem=send, recv_sem=recv,
            device_id=device, device_id_type=pl.DeviceIdType.MESH,
        )

    def both_ways(a, b, send, recv, k):
        return (
            push(a[0], a[1], send.at[0, k], recv.at[0, k], to_right),
            push(b[0], b[1], send.at[1, k], recv.at[1, k], to_left),
        )

    def start(copies):
        for copy in copies:
            copy.start()

    def arrive(copies):
        for copy in copies:
            copy.wait_recv()

    def early_out():
        a = (tok_ref.at[:, pl.ds(late, quarter - late)], xb.at[0, t])
        return both_ways(a, a, b1_send, b1_recv, 0)

    def early_in():
        a, b = xb.at[0, left], xb.at[0, right]
        return both_ways((a, a), (b, b), b1_send, b1_recv, 0)

    def early_pass(from_left, from_right):
        a = xb.at[0, from_left, pl.ds(0, rows // 2)]
        b = xb.at[0, from_right, pl.ds(rows // 2, rows // 2)]
        return both_ways((a, a), (b, b), b2_send, b2_recv, 0)

    meta_x = push(table.at[xh], table.at[xh], meta_send.at[0], meta_recv.at[0], partner)
    meta_s = push(table.at[xh], table.at[2], meta_send.at[1], meta_recv.at[1], (after, e, t))
    late_part = tok_ref.at[:, pl.ds(0, late)]
    tok_x = push(late_part, tok2.at[xh], tok_send, tok_recv, partner)
    meta_x.start()
    tok_x.start()
    start(early_out())
    meta_s.start()
    tok2[xh] = tok_ref[:, :late]
    xb[0, t] = tok_ref[:, late:]

    earlier = (iota((rows, rows), 0) < iota((rows, rows), 1)).astype(BF16)

    def slots_by_expert(gates):
        names = (gates > 0).astype(F32)
        return jnp.where(names > 0, dot(names.astype(BF16), earlier), -1000.0)

    slot_t[xh] = slots_by_expert(own)
    push(table.at[1 - xh], table.at[1 - xh], meta_send.at[0], meta_recv.at[0], partner).wait_recv()
    slot_t[1 - xh] = slots_by_expert(table[1 - xh])
    arrive(early_in())
    start(early_pass(left, right))

    def to_z(k):
        return push(xs.at[k], xg.at[k, t], z_send.at[k], z_recv.at[k], (sec, z_to(k) * 2 + xh, t))

    def slots_to_z(k):
        return push(
            slot_out.at[k], slot_in.at[k], slot_send.at[k], slot_recv.at[k],
            (sec, z_to(k) * 2 + xh, t),
        )

    def picked(slots, shift, count):
        return (slots + shift == iota((count, rows), 0).astype(F32)).astype(BF16)

    def pick(k):
        expert = z_to(k) * 2 + xh
        chosen = [picked(slot_t[j, pl.ds(expert, 1), :], float(CAP * j), pair) for j in range(2)]
        return (dot(chosen[0], tok2[0]) + dot(chosen[1], tok2[1])).astype(BF16)

    def gather(k):
        a = xg.at[k, t]
        return both_ways((a, a), (a, a), g1_send, g1_recv, k)

    def gathered(k):
        a, b = xg.at[k, left], xg.at[k, right]
        return both_ways((a, a), (b, b), g1_send, g1_recv, k)

    def forward(k, from_left, from_right):
        a = xg.at[k, from_left, :, pl.ds(0, late // 2)]
        b = xg.at[k, from_right, :, pl.ds(late // 2, late // 2)]
        return both_ways((a, a), (b, b), g2_send, g2_recv, k)

    push(late_part, tok2.at[1 - xh], tok_send, tok_recv, partner).wait_recv()
    xg[0, t] = pick(0)
    start(gather(0))

    def ring_next(k):
        dz = 2 * lax.rem(k, 2) - 1
        device = (sec, lax.rem(z + dz + nz, nz) * 2 + xh, t)
        return push(xb.at[k], xb.at[k + 2], ring_send.at[k], ring_recv.at[k + 2], device)

    up_z, down_z = (sec, lax.rem(z + 1, nz) * 2 + xh, t), (sec, lax.rem(z + nz - 1, nz) * 2 + xh, t)

    def ring_first():
        return (
            push(xb.at[0], xb.at[1], ring_send.at[nz - 2], ring_recv.at[1], up_z),
            push(xb.at[0], xb.at[2], ring_send.at[nz - 1], ring_recv.at[2], down_z),
        )

    def ring_in(k):
        return push(xb.at[0], xb.at[k], ring_send.at[0], ring_recv.at[k], up_z)

    def ring_last(j):
        part = pl.ds(j * (ny // 2), ny // 2)
        return push(
            xb.at[nz - 3 + j, part], xb.at[nz - 1, part], tail_send.at[j], tail_recv.at[j],
            (up_z, down_z)[j],
        )

    def over_x(k):
        return push(px.at[k], pr.at[k], x_send.at[k], x_recv.at[k], partner)

    def pick_for_partner(k):
        chosen = picked(slot_in[k, pl.ds(1 - xh, 1), :], ((PAD - CAP) * xh).astype(F32), PAD)
        for q in range(ny):
            px[k, q] = dot(chosen, xb[k, q]).astype(BF16)
        over_x(k).start()

    slot_in[0, 0:1, :] = slot_t[xh, pl.ds(z * 2, 1), :]
    slot_in[0, 1:2, :] = slot_t[xh, pl.ds(z * 2 + 1, 1), :]
    arrive(early_pass(opposite, opposite))
    start(ring_first())

    def send_z(k, carry):
        xs[k] = pick(k)
        for j in range(2):
            slot_out[k, j : j + 1, :] = slot_t[xh, pl.ds(z_to(k) * 2 + j, 1), :]
        slots_to_z(k).start()
        to_z(k).start()
        return carry

    lax.fori_loop(1, nz, send_z, 0)
    pick_for_partner(0)

    push(table.at[2], table.at[2], meta_send.at[1], meta_recv.at[1], (after, e, t)).wait_recv()
    filler = jnp.zeros((128 - NAMES, rows), F32)
    gates = jnp.transpose(jnp.concatenate([table[2], filler], axis=0))
    slots = jnp.transpose(jnp.concatenate([slots_by_expert(table[2]), filler], axis=0))
    lanes = iota((rows, 128), 1)
    place = iota((rows, 2 * PAD), 1).astype(F32)

    def build_mix(k, carry):
        total = jnp.zeros((rows, 2 * PAD), F32)
        for j in range(2):
            here = lanes == z_to(k) * 2 + j
            gate = jnp.sum(jnp.where(here, gates, 0.0), axis=1, keepdims=True)
            slot = jnp.sum(jnp.where(here, slots, 0.0), axis=1, keepdims=True)
            at = slot + ((PAD - CAP) * xh).astype(F32) + float(PAD * j)
            total = total + jnp.where(place == at, gate, 0.0)
        high = total.astype(BF16)
        mix[k, 0] = high
        mix[k, 1] = (total - high.astype(F32)).astype(BF16)
        return carry

    lax.fori_loop(0, nz, build_mix, 0)
    acc[...] = jnp.zeros_like(acc)

    for load in loads:
        load.wait()

    def relay(k):
        return both_ways((s1.at[0, k], r1.at[0, k]), (s1.at[1, k], r1.at[1, k]), r1_send, r1_recv, k)

    def direct(k):
        return both_ways((s2.at[0, k], r2.at[0, k]), (s2.at[1, k], r2.at[1, k]), r2_send, r2_recv, k)

    def joined(k):
        return both_ways((s3.at[0, k], r3.at[0, k]), (s3.at[1, k], r3.at[1, k]), r3_send, r3_recv, k)

    def give_back(k):
        return tuple(
            push(
                ret.at[k, pl.ds((pair - PAD) * j, PAD)], back.at[k, pl.ds(PAD * xh, PAD)],
                back_send.at[j, k], back_recv.at[xh, k], (after, z_from(k) * 2 + j, t),
            )
            for j in range(2)
        )

    def given_back(k):
        return tuple(
            push(
                ret.at[k, pl.ds((pair - PAD) * j, PAD)], back.at[k, pl.ds(PAD * j, PAD)],
                back_send.at[j, k], back_recv.at[j, k], to_right,
            )
            for j in range(2)
        )

    def ring_stage(k):
        @pl.when(k < nz - 1)
        def _():
            ring_in(k).wait_recv()

        @pl.when(k < nz - 3)
        def _():
            ring_next(k).start()

        for j in range(2):
            @pl.when(k == nz - 3 + j)
            def _(j=j):
                ring_last(j).start()

        @pl.when(k == nz - 1)
        def _():
            ring_last(0).wait_recv()
            ring_last(1).wait_recv()

        slots_to_z(k).wait_recv()
        pick_for_partner(k)

    def gather_stage(k):
        push(xs.at[k], xg.at[k, t], z_send.at[k], z_recv.at[k], to_right).wait_recv()
        start(gather(k))

    def forward_stage(k):
        arrive(gathered(k))
        start(forward(k, left, right))

    def up_stage(k):
        arrive(forward(k, opposite, opposite))
        over_x(k).wait_recv()
        chosen = picked(slot_in[k, pl.ds(xh, 1), :], (CAP * xh).astype(F32), pair)
        theirs = pl.ds(pl.multiple_of((pair - PAD) * (1 - xh), 16), PAD)
        for q in range(ny):
            x1[q] = dot(chosen, xb[k, q]).astype(BF16)
            x1[q, theirs] = x1[q, theirs] + pr[k, q]
        gate_act = up_act = None
        for q in range(ny):
            for x, first, count in (
                (xg[k, q], q * quarter, late), (x1[q], q * quarter + late, quarter - late)
            ):
                g = dot(x, wg[first : first + count, :])
                u = dot(x, wu[first : first + count, :])
                gate_act = g if gate_act is None else gate_act + g
                up_act = u if up_act is None else up_act + u
        hidden[k] = (gate_act / (1.0 + jnp.exp(-gate_act)) * up_act).astype(BF16)
        part = dot(hidden[k], wd[opposite]).astype(BF16)
        s1[0, k] = part[:, :half]
        s1[1, k] = part[:, half:]
        start(relay(k))
        s2[0, k] = dot(hidden[k], wd[right, :, half:]).astype(BF16)
        s2[1, k] = dot(hidden[k], wd[left, :, :half]).astype(BF16)
        start(direct(k))

    def down_stage(k):
        arrive(relay(k))
        h = hidden[k]
        s3[0, k] = (dot(h, wd[right, :, :half]) + r1[0, k].astype(F32)).astype(BF16)
        s3[1, k] = (dot(h, wd[left, :, half:]) + r1[1, k].astype(F32)).astype(BF16)
        start(joined(k))

    def sum_stage(k):
        arrive(direct(k))
        arrive(joined(k))
        part = dot(hidden[k], wd[t])
        ret[k, :, :half] = (part[:, :half] + r3[0, k].astype(F32) + r2[1, k].astype(F32)).astype(BF16)
        ret[k, :, half:] = (part[:, half:] + r2[0, k].astype(F32) + r3[1, k].astype(F32)).astype(BF16)
        start(give_back(k))

    def mix_stage(k):
        arrive(given_back(k))
        y = back[k]
        acc[...] += dot(mix[k, 0], y) + dot(mix[k, 1], y)

    stages = (
        (-2, gather_stage, 1),
        (-2, ring_stage, 1),
        (-1, forward_stage, 0),
        (0, up_stage, 0),
        (1, down_stage, 0),
        (2, sum_stage, 0),
        (4, mix_stage, 0),
    )

    def step(i, carry):
        for lag, stage, first in stages:
            k = i - lag

            @pl.when((k >= first) & (k < nz))
            def _(stage=stage, k=k):
                stage(k)

        return carry

    lax.fori_loop(-1, nz + 4, step, 0)
    out_ref[...] = acc[...].astype(out_ref.dtype)

    def leave(copies):
        for copy in copies:
            copy.wait_send()

    leave((meta_x, meta_s, tok_x))
    leave(early_out())
    leave(early_pass(left, right))
    leave(ring_first())
    leave((ring_last(0), ring_last(1)))

    def drain(k, carry):
        @pl.when(k > 0)
        def _():
            leave((to_z(k), slots_to_z(k)))

        @pl.when((k > 0) & (k < nz - 3))
        def _():
            ring_next(k).wait_send()

        for copies in (
            gather(k), forward(k, left, right), relay(k), direct(k), joined(k), give_back(k),
        ):
            leave(copies)
        over_x(k).wait_send()
        return carry

    lax.fori_loop(0, nz, drain, 0)


def on_device(nsec, nz, ny, tokens, expert_ids, gate_values, w_gate, w_up, w_down):
    rows, quarter = tokens.shape[1:]
    width, units = w_gate.shape[2:]
    pair, half = 2 * CAP, quarter // 2
    late = 3 * quarter // 4
    early = quarter - late
    dma = pltpu.SemaphoreType.DMA
    vmem = lambda *shape, dtype=BF16: pltpu.VMEM(shape, dtype)
    sides = lambda n: [dma((2, n)), dma((2, n))]
    each = lambda n: [dma((n,)), dma((n,))]
    combined = pl.pallas_call(
        functools.partial(moe_kernel, nsec, nz, ny),
        out_shape=jax.ShapeDtypeStruct((rows, quarter), BF16),
        in_specs=[pl.BlockSpec(memory_space=pltpu.VMEM)] * 3 + [pl.BlockSpec(memory_space=pl.ANY)] * 3,
        out_specs=pl.BlockSpec(memory_space=pltpu.VMEM),
        scratch_shapes=[
            vmem(width, units), vmem(width, units), vmem(ny, units, quarter),
            vmem(3, NAMES, rows, dtype=F32),
            vmem(2, NAMES, rows, dtype=F32),
            vmem(2, rows, late),
            vmem(nz, pair, late),
            vmem(nz, ny, pair, late),
            vmem(nz, 8, rows, dtype=F32), vmem(nz, 8, rows, dtype=F32),
            vmem(nz, ny, rows, early),
            vmem(nz, ny, PAD, early), vmem(nz, ny, PAD, early),
            vmem(ny, pair, early),
            vmem(nz, pair, units),
            vmem(2, nz, pair, half), vmem(2, nz, pair, half),
            vmem(2, nz, pair, half), vmem(2, nz, pair, half),
            vmem(2, nz, pair, half), vmem(2, nz, pair, half),
            vmem(nz, pair, quarter),
            vmem(nz, 2 * PAD, quarter),
            vmem(nz, 2, rows, 2 * PAD),
            vmem(rows, quarter, dtype=F32),
            dma((2 + ny,)), *each(2), dma, dma, *each(nz), *each(nz),
            *sides(1), *sides(1), *each(nz), *each(2), *each(nz),
            *sides(nz), *sides(nz), *sides(nz), *sides(nz), *sides(nz),
            *sides(nz),
        ],
        compiler_params=pltpu.CompilerParams(
            collective_id=0, has_side_effects=True, vmem_limit_bytes=60 * 1024 * 1024
        ),
        cost_estimate=pl.CostEstimate(
            flops=6 * nz * pair * width * units, bytes_accessed=6 * width * units, transcendentals=0
        ),
    )(tokens[0], expert_ids[0].T, gate_values[0].T, w_gate[0, 0], w_up[0, 0], w_down[0, 0])
    return combined[None]


def solution(mesh):
    nsec, nexp, ny = mesh.shape["section"], mesh.shape["expert"], mesh.shape["tensor"]
    in_specs = (
        P("section", "expert", "tensor"),
        P("section", "expert", None),
        P("section", "expert", None),
        P("section", "expert", None, "tensor"),
        P("section", "expert", None, "tensor"),
        P("section", "expert", "tensor", None),
    )
    return jax.shard_map(
        functools.partial(on_device, nsec, nexp // 2, ny),
        mesh=mesh, in_specs=in_specs, out_specs=P("section", "expert", "tensor"), check_vma=False,
    )
```

```python
import functools

import jax
import jax.numpy as jnp
from jax import lax
from jax.experimental import pallas as pl
from jax.experimental.pallas import tpu as pltpu
from jax.sharding import PartitionSpec as P

CAP = 72
PAD = 80
NAMES = 16
BF16 = jnp.bfloat16
F32 = jnp.float32


def iota(shape, dim):
    return lax.broadcasted_iota(jnp.int32, shape, dim)


def dot(a, b):
    return jnp.dot(a, b, preferred_element_type=F32)


def order_of(nz):
    return {2: (0, 1), 4: (0, 1, 3, 2), 8: (0, 1, 3, 6, 7, 5, 4, 2)}[nz]


def moe_kernel(
    nsec, nz, ny,
    tok_ref, ids_ref, gate_ref, wg_hbm, wu_hbm, wd_hbm, out_ref,
    wg, wu, wd, table, slot_t, tok2, xs, xg, slot_out, slot_in, xb, px, pr, x1, hidden,
    s1, r1, s2, r2, s3, r3, ret, back, mix, acc,
    w_sem, meta_send, meta_recv, tok_send, tok_recv, z_send, z_recv, slot_send, slot_recv,
    b1_send, b1_recv, b2_send, b2_recv, ring_send, ring_recv, tail_send, tail_recv, x_send, x_recv,
    g1_send, g1_recv, g2_send, g2_recv, r1_send, r1_recv, r2_send, r2_recv, r3_send, r3_recv,
    back_send, back_recv,
):
    sec, e, t = lax.axis_index("section"), lax.axis_index("expert"), lax.axis_index("tensor")
    z, xh = lax.div(e, 2), lax.rem(e, 2)
    rows, quarter = tok_ref.shape
    half = quarter // 2
    late = xg.shape[3]
    pair = 2 * CAP
    right, left, opposite = lax.rem(t + 1, ny), lax.rem(t + ny - 1, ny), lax.rem(t + 2, ny)
    after, before = lax.rem(sec + 1, nsec), lax.rem(sec + nsec - 1, nsec)

    def away(k):
        return lax.rem(lax.div(k + 1, 2) * (2 * lax.rem(k, 2) - 1) + nz, nz)

    def z_to(k):
        return lax.rem(z + away(k), nz)

    def z_from(k):
        return lax.rem(z - away(k) + nz, nz)

    order = order_of(nz)
    packed = sum(k << (3 * p) for p, k in enumerate(order))

    def chunk_at(p):
        return lax.rem(lax.shift_right_logical(packed, 3 * p), 8)

    loads = [
        pltpu.make_async_copy(wg_hbm, wg, w_sem.at[0]),
        pltpu.make_async_copy(wu_hbm, wu, w_sem.at[1]),
    ] + [
        pltpu.make_async_copy(wd_hbm.at[:, pl.ds(q * quarter, quarter)], wd.at[q], w_sem.at[2 + q])
        for q in range(ny)
    ]
    for load in loads:
        load.start()

    named = iota((NAMES, rows), 0)
    own = jnp.zeros((NAMES, rows), F32)
    for k in range(ids_ref.shape[0]):
        own = own + jnp.where(ids_ref[k : k + 1, :] == named, gate_ref[k : k + 1, :], 0.0)
    table[xh] = own

    barrier = pltpu.get_barrier_semaphore()

    def greet(device):
        pl.semaphore_signal(barrier, inc=1, device_id=device, device_id_type=pl.DeviceIdType.MESH)

    partner = (sec, z * 2 + 1 - xh, t)
    to_right, to_left = (sec, e, right), (sec, e, left)
    greet(to_right)
    greet(to_left)
    greet(partner)
    for k in range(1, nz):
        greet((sec, z_from(k) * 2 + xh, t))
    for other in range(2 * nz):
        greet((before, other, t))
    pl.semaphore_wait(barrier, (nz - 1) + 3 + 2 * nz)

    def push(src, dst, send, recv, device):
        return pltpu.make_async_remote_copy(
            src_ref=src, dst_ref=dst, send_sem=send, recv_sem=recv,
            device_id=device, device_id_type=pl.DeviceIdType.MESH,
        )

    def both_ways(a, b, send, recv, k):
        return (
            push(a[0], a[1], send.at[0, k], recv.at[0, k], to_right),
            push(b[0], b[1], send.at[1, k], recv.at[1, k], to_left),
        )

    def start(copies):
        for copy in copies:
            copy.start()

    def arrive(copies):
        for copy in copies:
            copy.wait_recv()

    def early_out():
        a = (tok_ref.at[:, pl.ds(late, quarter - late)], xb.at[0, t])
        return both_ways(a, a, b1_send, b1_recv, 0)

    def early_in():
        a, b = xb.at[0, left], xb.at[0, right]
        return both_ways((a, a), (b, b), b1_send, b1_recv, 0)

    def early_pass(from_left, from_right):
        a = xb.at[0, from_left, pl.ds(0, rows // 2)]
        b = xb.at[0, from_right, pl.ds(rows // 2, rows // 2)]
        return both_ways((a, a), (b, b), b2_send, b2_recv, 0)

    meta_x = push(table.at[xh], table.at[xh], meta_send.at[0], meta_recv.at[0], partner)
    meta_s = push(table.at[xh], table.at[2], meta_send.at[1], meta_recv.at[1], (after, e, t))
    late_part = tok_ref.at[:, pl.ds(0, late)]
    tok_x = push(late_part, tok2.at[xh], tok_send, tok_recv, partner)
    meta_x.start()
    tok_x.start()
    start(early_out())
    meta_s.start()
    tok2[xh] = tok_ref[:, :late]
    xb[0, t] = tok_ref[:, late:]

    earlier = (iota((rows, rows), 0) < iota((rows, rows), 1)).astype(BF16)

    def slots_by_expert(gates):
        names = (gates > 0).astype(F32)
        return jnp.where(names > 0, dot(names.astype(BF16), earlier), -1000.0)

    slot_t[xh] = slots_by_expert(own)
    push(table.at[1 - xh], table.at[1 - xh], meta_send.at[0], meta_recv.at[0], partner).wait_recv()
    slot_t[1 - xh] = slots_by_expert(table[1 - xh])
    arrive(early_in())
    start(early_pass(left, right))

    def to_z(k):
        return push(xs.at[k], xg.at[k, t], z_send.at[k], z_recv.at[k], (sec, z_to(k) * 2 + xh, t))

    def slots_to_z(k):
        return push(
            slot_out.at[k], slot_in.at[k], slot_send.at[k], slot_recv.at[k],
            (sec, z_to(k) * 2 + xh, t),
        )

    def picked(slots, shift, count):
        return (slots + shift == iota((count, rows), 0).astype(F32)).astype(BF16)

    def pick(k):
        expert = z_to(k) * 2 + xh
        chosen = [picked(slot_t[j, pl.ds(expert, 1), :], float(CAP * j), pair) for j in range(2)]
        return (dot(chosen[0], tok2[0]) + dot(chosen[1], tok2[1])).astype(BF16)

    def gather(k):
        a = xg.at[k, t]
        return both_ways((a, a), (a, a), g1_send, g1_recv, k)

    def gathered(k):
        a, b = xg.at[k, left], xg.at[k, right]
        return both_ways((a, a), (b, b), g1_send, g1_recv, k)

    def forward(k, from_left, from_right):
        a = xg.at[k, from_left, :, pl.ds(0, late // 2)]
        b = xg.at[k, from_right, :, pl.ds(late // 2, late // 2)]
        return both_ways((a, a), (b, b), g2_send, g2_recv, k)

    push(late_part, tok2.at[1 - xh], tok_send, tok_recv, partner).wait_recv()
    xg[0, t] = pick(0)
    start(gather(0))

    def ring_next(k):
        dz = 2 * lax.rem(k, 2) - 1
        device = (sec, lax.rem(z + dz + nz, nz) * 2 + xh, t)
        return push(xb.at[k], xb.at[k + 2], ring_send.at[k], ring_recv.at[k + 2], device)

    up_z, down_z = (sec, lax.rem(z + 1, nz) * 2 + xh, t), (sec, lax.rem(z + nz - 1, nz) * 2 + xh, t)

    def ring_first():
        return (
            push(xb.at[0], xb.at[1], ring_send.at[nz - 2], ring_recv.at[1], up_z),
            push(xb.at[0], xb.at[2], ring_send.at[nz - 1], ring_recv.at[2], down_z),
        )

    def ring_in(k):
        return push(xb.at[0], xb.at[k], ring_send.at[0], ring_recv.at[k], up_z)

    def ring_last(j):
        part = pl.ds(j * (ny // 2), ny // 2)
        return push(
            xb.at[nz - 3 + j, part], xb.at[nz - 1, part], tail_send.at[j], tail_recv.at[j],
            (up_z, down_z)[j],
        )

    def over_x(k):
        return push(px.at[k], pr.at[k], x_send.at[k], x_recv.at[k], partner)

    def pick_for_partner(k):
        chosen = picked(slot_in[k, pl.ds(1 - xh, 1), :], ((PAD - CAP) * xh).astype(F32), PAD)
        for q in range(ny):
            px[k, q] = dot(chosen, xb[k, q]).astype(BF16)
        over_x(k).start()

    slot_in[0, 0:1, :] = slot_t[xh, pl.ds(z * 2, 1), :]
    slot_in[0, 1:2, :] = slot_t[xh, pl.ds(z * 2 + 1, 1), :]
    arrive(early_pass(opposite, opposite))
    start(ring_first())

    def send_stage(k):
        xs[k] = pick(k)
        to_z(k).start()

    def send_slots(k, carry):
        for j in range(2):
            slot_out[k, j : j + 1, :] = slot_t[xh, pl.ds(z_to(k) * 2 + j, 1), :]
        slots_to_z(k).start()
        return carry

    for p in (1, 2):
        if p < nz:
            send_stage(jnp.int32(order[p]))
    lax.fori_loop(1, nz, send_slots, 0)
    pick_for_partner(0)

    for load in loads:
        load.wait()

    def build_all_mix():
        push(table.at[2], table.at[2], meta_send.at[1], meta_recv.at[1], (after, e, t)).wait_recv()
        filler = jnp.zeros((128 - NAMES, rows), F32)
        gates = jnp.transpose(jnp.concatenate([table[2], filler], axis=0))
        slots = jnp.transpose(jnp.concatenate([slots_by_expert(table[2]), filler], axis=0))
        lanes = iota((rows, 128), 1)
        place = iota((rows, 2 * PAD), 1).astype(F32)

        def build_mix(k, carry):
            total = jnp.zeros((rows, 2 * PAD), F32)
            for j in range(2):
                here = lanes == z_to(k) * 2 + j
                gate = jnp.sum(jnp.where(here, gates, 0.0), axis=1, keepdims=True)
                slot = jnp.sum(jnp.where(here, slots, 0.0), axis=1, keepdims=True)
                at = slot + ((PAD - CAP) * xh).astype(F32) + float(PAD * j)
                total = total + jnp.where(place == at, gate, 0.0)
            high = total.astype(BF16)
            mix[k, 0] = high
            mix[k, 1] = (total - high.astype(F32)).astype(BF16)
            return carry

        lax.fori_loop(0, nz, build_mix, 0)
        acc[...] = jnp.zeros_like(acc)

    def relay(k):
        return both_ways((s1.at[0, k], r1.at[0, k]), (s1.at[1, k], r1.at[1, k]), r1_send, r1_recv, k)

    def direct(k):
        return both_ways((s2.at[0, k], r2.at[0, k]), (s2.at[1, k], r2.at[1, k]), r2_send, r2_recv, k)

    def joined(k):
        return both_ways((s3.at[0, k], r3.at[0, k]), (s3.at[1, k], r3.at[1, k]), r3_send, r3_recv, k)

    def give_back(k):
        return tuple(
            push(
                ret.at[k, pl.ds((pair - PAD) * j, PAD)], back.at[k, pl.ds(PAD * xh, PAD)],
                back_send.at[j, k], back_recv.at[xh, k], (after, z_from(k) * 2 + j, t),
            )
            for j in range(2)
        )

    def given_back(k):
        return tuple(
            push(
                ret.at[k, pl.ds((pair - PAD) * j, PAD)], back.at[k, pl.ds(PAD * j, PAD)],
                back_send.at[j, k], back_recv.at[j, k], to_right,
            )
            for j in range(2)
        )

    def ring_stage(k):
        @pl.when(k < nz - 1)
        def _():
            ring_in(k).wait_recv()

        @pl.when(k < nz - 3)
        def _():
            ring_next(k).start()

        for j in range(2):
            @pl.when(k == nz - 3 + j)
            def _(j=j):
                ring_last(j).start()

        @pl.when(k == nz - 1)
        def _():
            ring_last(0).wait_recv()
            ring_last(1).wait_recv()

        slots_to_z(k).wait_recv()
        pick_for_partner(k)

    def gather_stage(k):
        push(xs.at[k], xg.at[k, t], z_send.at[k], z_recv.at[k], to_right).wait_recv()
        start(gather(k))

    def forward_stage(k):
        arrive(gathered(k))
        start(forward(k, left, right))

    def up_stage(k):
        arrive(forward(k, opposite, opposite))
        over_x(k).wait_recv()
        chosen = picked(slot_in[k, pl.ds(xh, 1), :], (CAP * xh).astype(F32), pair)
        theirs = pl.ds(pl.multiple_of((pair - PAD) * (1 - xh), 16), PAD)
        for q in range(ny):
            x1[q] = dot(chosen, xb[k, q]).astype(BF16)
            x1[q, theirs] = x1[q, theirs] + pr[k, q]
        gate_act = up_act = None
        for q in range(ny):
            for x, first, count in (
                (xg[k, q], q * quarter, late), (x1[q], q * quarter + late, quarter - late)
            ):
                g = dot(x, wg[first : first + count, :])
                u = dot(x, wu[first : first + count, :])
                gate_act = g if gate_act is None else gate_act + g
                up_act = u if up_act is None else up_act + u
        hidden[k] = (gate_act / (1.0 + jnp.exp(-gate_act)) * up_act).astype(BF16)
        part = dot(hidden[k], wd[opposite]).astype(BF16)
        s1[0, k] = part[:, :half]
        s1[1, k] = part[:, half:]
        start(relay(k))
        s2[0, k] = dot(hidden[k], wd[right, :, half:]).astype(BF16)
        s2[1, k] = dot(hidden[k], wd[left, :, :half]).astype(BF16)
        start(direct(k))

    def down_stage(k):
        arrive(relay(k))
        h = hidden[k]
        s3[0, k] = (dot(h, wd[right, :, :half]) + r1[0, k].astype(F32)).astype(BF16)
        s3[1, k] = (dot(h, wd[left, :, half:]) + r1[1, k].astype(F32)).astype(BF16)
        start(joined(k))

    def sum_stage(k):
        arrive(direct(k))
        arrive(joined(k))
        part = dot(hidden[k], wd[t])
        ret[k, :, :half] = (part[:, :half] + r3[0, k].astype(F32) + r2[1, k].astype(F32)).astype(BF16)
        ret[k, :, half:] = (part[:, half:] + r2[0, k].astype(F32) + r3[1, k].astype(F32)).astype(BF16)
        start(give_back(k))

    def mix_stage(k):
        arrive(given_back(k))
        y = back[k]
        acc[...] += dot(mix[k, 0], y) + dot(mix[k, 1], y)

    def leave(copies):
        for copy in copies:
            copy.wait_send()

    def drain_stage(k):
        @pl.when(k > 0)
        def _():
            leave((to_z(k), slots_to_z(k)))

        @pl.when((k > 0) & (k < nz - 3))
        def _():
            ring_next(k).wait_send()

        for copies in (
            gather(k), forward(k, left, right), relay(k), direct(k), joined(k), give_back(k),
        ):
            leave(copies)
        over_x(k).wait_send()

    def staged(i, lag, stage, first):
        p = i - lag

        @pl.when((p >= first) & (p < nz))
        def _():
            stage(chunk_at(p))

    def step(i, carry):
        staged(i, -2, gather_stage, 1)
        staged(i, -1, forward_stage, 0)
        staged(i, 0, up_stage, 0)
        staged(i, 1, down_stage, 0)

        @pl.when((i >= 0) & (i < nz // 2))
        def _():
            ring_stage(2 * i + 1)

        @pl.when((i >= 0) & (i < nz // 2 - 1))
        def _():
            ring_stage(2 * i + 2)

        staged(i, -4, send_stage, 3)

        @pl.when(i == 0)
        def _():
            build_all_mix()

        staged(i, 2, sum_stage, 0)
        staged(i, 4, mix_stage, 0)
        staged(i, 5, drain_stage, 0)
        return carry

    lax.fori_loop(-1, nz + 5, step, 0)
    out_ref[...] = acc[...].astype(out_ref.dtype)

    leave((meta_x, meta_s, tok_x))
    leave(early_out())
    leave(early_pass(left, right))
    leave(ring_first())
    leave((ring_last(0), ring_last(1)))


def on_device(nsec, nz, ny, tokens, expert_ids, gate_values, w_gate, w_up, w_down):
    rows, quarter = tokens.shape[1:]
    width, units = w_gate.shape[2:]
    pair, half = 2 * CAP, quarter // 2
    late = quarter // 4
    early = quarter - late
    dma = pltpu.SemaphoreType.DMA
    vmem = lambda *shape, dtype=BF16: pltpu.VMEM(shape, dtype)
    sides = lambda n: [dma((2, n)), dma((2, n))]
    each = lambda n: [dma((n,)), dma((n,))]
    combined = pl.pallas_call(
        functools.partial(moe_kernel, nsec, nz, ny),
        out_shape=jax.ShapeDtypeStruct((rows, quarter), BF16),
        in_specs=[pl.BlockSpec(memory_space=pltpu.VMEM)] * 3 + [pl.BlockSpec(memory_space=pl.ANY)] * 3,
        out_specs=pl.BlockSpec(memory_space=pltpu.VMEM),
        scratch_shapes=[
            vmem(width, units), vmem(width, units), vmem(ny, units, quarter),
            vmem(3, NAMES, rows, dtype=F32),
            vmem(2, NAMES, rows, dtype=F32),
            vmem(2, rows, late),
            vmem(nz, pair, late),
            vmem(nz, ny, pair, late),
            vmem(nz, 8, rows, dtype=F32), vmem(nz, 8, rows, dtype=F32),
            vmem(nz, ny, rows, early),
            vmem(nz, ny, PAD, early), vmem(nz, ny, PAD, early),
            vmem(ny, pair, early),
            vmem(nz, pair, units),
            vmem(2, nz, pair, half), vmem(2, nz, pair, half),
            vmem(2, nz, pair, half), vmem(2, nz, pair, half),
            vmem(2, nz, pair, half), vmem(2, nz, pair, half),
            vmem(nz, pair, quarter),
            vmem(nz, 2 * PAD, quarter),
            vmem(nz, 2, rows, 2 * PAD),
            vmem(rows, quarter, dtype=F32),
            dma((2 + ny,)), *each(2), dma, dma, *each(nz), *each(nz),
            *sides(1), *sides(1), *each(nz), *each(2), *each(nz),
            *sides(nz), *sides(nz), *sides(nz), *sides(nz), *sides(nz),
            *sides(nz),
        ],
        compiler_params=pltpu.CompilerParams(
            collective_id=0, has_side_effects=True, vmem_limit_bytes=60 * 1024 * 1024
        ),
        cost_estimate=pl.CostEstimate(
            flops=6 * nz * pair * width * units, bytes_accessed=6 * width * units, transcendentals=0
        ),
    )(tokens[0], expert_ids[0].T, gate_values[0].T, w_gate[0, 0], w_up[0, 0], w_down[0, 0])
    return combined[None]


def solution(mesh):
    nsec, nexp, ny = mesh.shape["section"], mesh.shape["expert"], mesh.shape["tensor"]
    in_specs = (
        P("section", "expert", "tensor"),
        P("section", "expert", None),
        P("section", "expert", None),
        P("section", "expert", None, "tensor"),
        P("section", "expert", None, "tensor"),
        P("section", "expert", "tensor", None),
    )
    return jax.shard_map(
        functools.partial(on_device, nsec, nexp // 2, ny),
        mesh=mesh, in_specs=in_specs, out_specs=P("section", "expert", "tensor"), check_vma=False,
    )
```

```python
import functools

import jax
import jax.numpy as jnp
from jax import lax
from jax.experimental import pallas as pl
from jax.experimental.pallas import tpu as pltpu
from jax.sharding import PartitionSpec as P

CAP = 72
PAD = 80
NAMES = 16
BF16 = jnp.bfloat16
F32 = jnp.float32


def iota(shape, dim):
    return lax.broadcasted_iota(jnp.int32, shape, dim)


def dot(a, b):
    return jnp.dot(a, b, preferred_element_type=F32)


def order_of(nz):
    return {2: (0, 1), 4: (0, 1, 3, 2), 8: (0, 1, 4, 5, 6, 3, 7, 2)}[nz]


def moe_kernel(
    nsec, nz, ny,
    tok_ref, ids_ref, gate_ref, wg_hbm, wu_hbm, wd_hbm, out_ref,
    wg, wu, wd, table, slot_t, tok2, xs, xg, slot_out, slot_in, xb, px, pr, x1, hidden,
    s1, r1, s2, r2, s3, r3, ret, back, mix, acc,
    w_sem, meta_send, meta_recv, tok_send, tok_recv, z_send, z_recv, slot_send, slot_recv,
    b1_send, b1_recv, b2_send, b2_recv, ring_send, ring_recv, tail_send, tail_recv, x_send, x_recv,
    g1_send, g1_recv, g2_send, g2_recv, r1_send, r1_recv, r2_send, r2_recv, r3_send, r3_recv,
    back_send, back_recv,
):
    sec, e, t = lax.axis_index("section"), lax.axis_index("expert"), lax.axis_index("tensor")
    z, xh = lax.div(e, 2), lax.rem(e, 2)
    rows, quarter = tok_ref.shape
    half = quarter // 2
    late = xg.shape[3]
    pair = 2 * CAP
    right, left, opposite = lax.rem(t + 1, ny), lax.rem(t + ny - 1, ny), lax.rem(t + 2, ny)
    after, before = lax.rem(sec + 1, nsec), lax.rem(sec + nsec - 1, nsec)

    def away(k):
        return lax.rem(lax.div(k + 1, 2) * (2 * lax.rem(k, 2) - 1) + nz, nz)

    def z_to(k):
        return lax.rem(z + away(k), nz)

    def z_from(k):
        return lax.rem(z - away(k) + nz, nz)

    order = order_of(nz)
    packed = sum(k << (3 * p) for p, k in enumerate(order))

    def chunk_at(p):
        return lax.rem(lax.shift_right_logical(packed, 3 * p), 8)

    loads = [
        pltpu.make_async_copy(wg_hbm, wg, w_sem.at[0]),
        pltpu.make_async_copy(wu_hbm, wu, w_sem.at[1]),
    ] + [
        pltpu.make_async_copy(wd_hbm.at[:, pl.ds(q * quarter, quarter)], wd.at[q], w_sem.at[2 + q])
        for q in range(ny)
    ]
    for load in loads:
        load.start()

    named = iota((NAMES, rows), 0)
    own = jnp.zeros((NAMES, rows), F32)
    for k in range(ids_ref.shape[0]):
        own = own + jnp.where(ids_ref[k : k + 1, :] == named, gate_ref[k : k + 1, :], 0.0)
    table[xh] = own

    barrier = pltpu.get_barrier_semaphore()

    def greet(device):
        pl.semaphore_signal(barrier, inc=1, device_id=device, device_id_type=pl.DeviceIdType.MESH)

    partner = (sec, z * 2 + 1 - xh, t)
    to_right, to_left = (sec, e, right), (sec, e, left)
    greet(to_right)
    greet(to_left)
    greet(partner)
    for k in range(1, nz):
        greet((sec, z_from(k) * 2 + xh, t))
    for other in range(2 * nz):
        greet((before, other, t))
    pl.semaphore_wait(barrier, (nz - 1) + 3 + 2 * nz)

    def push(src, dst, send, recv, device):
        return pltpu.make_async_remote_copy(
            src_ref=src, dst_ref=dst, send_sem=send, recv_sem=recv,
            device_id=device, device_id_type=pl.DeviceIdType.MESH,
        )

    def both_ways(a, b, send, recv, k):
        return (
            push(a[0], a[1], send.at[0, k], recv.at[0, k], to_right),
            push(b[0], b[1], send.at[1, k], recv.at[1, k], to_left),
        )

    def start(copies):
        for copy in copies:
            copy.start()

    def arrive(copies):
        for copy in copies:
            copy.wait_recv()

    def early_out():
        a = (tok_ref.at[:, pl.ds(late, quarter - late)], xb.at[0, t])
        return both_ways(a, a, b1_send, b1_recv, 0)

    def early_in():
        a, b = xb.at[0, left], xb.at[0, right]
        return both_ways((a, a), (b, b), b1_send, b1_recv, 0)

    def early_pass(from_left, from_right):
        a = xb.at[0, from_left, pl.ds(0, rows // 2)]
        b = xb.at[0, from_right, pl.ds(rows // 2, rows // 2)]
        return both_ways((a, a), (b, b), b2_send, b2_recv, 0)

    meta_x = push(table.at[xh], table.at[xh], meta_send.at[0], meta_recv.at[0], partner)
    meta_s = push(table.at[xh], table.at[2], meta_send.at[1], meta_recv.at[1], (after, e, t))
    late_part = tok_ref.at[:, pl.ds(0, late)]
    tok_x = push(late_part, tok2.at[xh], tok_send, tok_recv, partner)
    meta_x.start()
    tok_x.start()
    start(early_out())
    meta_s.start()
    tok2[xh] = tok_ref[:, :late]
    xb[0, t] = tok_ref[:, late:]

    earlier = (iota((rows, rows), 0) < iota((rows, rows), 1)).astype(BF16)

    def slots_by_expert(gates):
        names = (gates > 0).astype(F32)
        return jnp.where(names > 0, dot(names.astype(BF16), earlier), -1000.0)

    slot_t[xh] = slots_by_expert(own)
    push(table.at[1 - xh], table.at[1 - xh], meta_send.at[0], meta_recv.at[0], partner).wait_recv()
    slot_t[1 - xh] = slots_by_expert(table[1 - xh])
    arrive(early_in())
    start(early_pass(left, right))

    def to_z(k):
        return push(xs.at[k], xg.at[k, t], z_send.at[k], z_recv.at[k], (sec, z_to(k) * 2 + xh, t))

    def slots_to_z(k):
        return push(
            slot_out.at[k], slot_in.at[k], slot_send.at[k], slot_recv.at[k],
            (sec, z_to(k) * 2 + xh, t),
        )

    def picked(slots, shift, count):
        return (slots + shift == iota((count, rows), 0).astype(F32)).astype(BF16)

    def pick(k):
        expert = z_to(k) * 2 + xh
        chosen = [picked(slot_t[j, pl.ds(expert, 1), :], float(CAP * j), pair) for j in range(2)]
        return (dot(chosen[0], tok2[0]) + dot(chosen[1], tok2[1])).astype(BF16)

    def gather(k):
        a = xg.at[k, t]
        return both_ways((a, a), (a, a), g1_send, g1_recv, k)

    def gathered(k):
        a, b = xg.at[k, left], xg.at[k, right]
        return both_ways((a, a), (b, b), g1_send, g1_recv, k)

    def forward(k, from_left, from_right):
        a = xg.at[k, from_left, :, pl.ds(0, late // 2)]
        b = xg.at[k, from_right, :, pl.ds(late // 2, late // 2)]
        return both_ways((a, a), (b, b), g2_send, g2_recv, k)

    push(late_part, tok2.at[1 - xh], tok_send, tok_recv, partner).wait_recv()
    xg[0, t] = pick(0)
    start(gather(0))

    def ring_next(k):
        dz = 2 * lax.rem(k, 2) - 1
        device = (sec, lax.rem(z + dz + nz, nz) * 2 + xh, t)
        return push(xb.at[k], xb.at[k + 2], ring_send.at[k], ring_recv.at[k + 2], device)

    up_z, down_z = (sec, lax.rem(z + 1, nz) * 2 + xh, t), (sec, lax.rem(z + nz - 1, nz) * 2 + xh, t)

    def ring_first():
        return (
            push(xb.at[0], xb.at[1], ring_send.at[nz - 2], ring_recv.at[1], up_z),
            push(xb.at[0], xb.at[2], ring_send.at[nz - 1], ring_recv.at[2], down_z),
        )

    def ring_in(k):
        return push(xb.at[0], xb.at[k], ring_send.at[0], ring_recv.at[k], up_z)

    def ring_last(j):
        part = pl.ds(j * (ny // 2), ny // 2)
        return push(
            xb.at[nz - 3 + j, part], xb.at[nz - 1, part], tail_send.at[j], tail_recv.at[j],
            (up_z, down_z)[j],
        )

    def over_x(k):
        return push(px.at[k], pr.at[k], x_send.at[k], x_recv.at[k], partner)

    def pick_for_partner(k):
        chosen = picked(slot_in[k, pl.ds(1 - xh, 1), :], ((PAD - CAP) * xh).astype(F32), PAD)
        for q in range(ny):
            px[k, q] = dot(chosen, xb[k, q]).astype(BF16)
        over_x(k).start()

    slot_in[0, 0:1, :] = slot_t[xh, pl.ds(z * 2, 1), :]
    slot_in[0, 1:2, :] = slot_t[xh, pl.ds(z * 2 + 1, 1), :]
    def send_stage(k):
        xs[k] = pick(k)
        to_z(k).start()

    for p in (1, 2):
        if p < nz:
            send_stage(jnp.int32(order[p]))

    arrive(early_pass(opposite, opposite))
    start(ring_first())

    def send_slots(k, carry):
        for j in range(2):
            slot_out[k, j : j + 1, :] = slot_t[xh, pl.ds(z_to(k) * 2 + j, 1), :]
        slots_to_z(k).start()
        return carry

    lax.fori_loop(1, nz, send_slots, 0)
    pick_for_partner(0)

    for load in loads:
        load.wait()

    def build_all_mix():
        push(table.at[2], table.at[2], meta_send.at[1], meta_recv.at[1], (after, e, t)).wait_recv()
        filler = jnp.zeros((128 - NAMES, rows), F32)
        gates = jnp.transpose(jnp.concatenate([table[2], filler], axis=0))
        slots = jnp.transpose(jnp.concatenate([slots_by_expert(table[2]), filler], axis=0))
        lanes = iota((rows, 128), 1)
        place = iota((rows, 2 * PAD), 1).astype(F32)

        def build_mix(k, carry):
            total = jnp.zeros((rows, 2 * PAD), F32)
            for j in range(2):
                here = lanes == z_to(k) * 2 + j
                gate = jnp.sum(jnp.where(here, gates, 0.0), axis=1, keepdims=True)
                slot = jnp.sum(jnp.where(here, slots, 0.0), axis=1, keepdims=True)
                at = slot + ((PAD - CAP) * xh).astype(F32) + float(PAD * j)
                total = total + jnp.where(place == at, gate, 0.0)
            high = total.astype(BF16)
            mix[k, 0] = high
            mix[k, 1] = (total - high.astype(F32)).astype(BF16)
            return carry

        lax.fori_loop(0, nz, build_mix, 0)
        acc[...] = jnp.zeros_like(acc)

    def relay(k):
        return both_ways((s1.at[0, k], r1.at[0, k]), (s1.at[1, k], r1.at[1, k]), r1_send, r1_recv, k)

    def direct(k):
        return both_ways((s2.at[0, k], r2.at[0, k]), (s2.at[1, k], r2.at[1, k]), r2_send, r2_recv, k)

    def joined(k):
        return both_ways((s3.at[0, k], r3.at[0, k]), (s3.at[1, k], r3.at[1, k]), r3_send, r3_recv, k)

    def give_back(k):
        return tuple(
            push(
                ret.at[k, pl.ds((pair - PAD) * j, PAD)], back.at[k, pl.ds(PAD * xh, PAD)],
                back_send.at[j, k], back_recv.at[xh, k], (after, z_from(k) * 2 + j, t),
            )
            for j in range(2)
        )

    def given_back(k):
        return tuple(
            push(
                ret.at[k, pl.ds((pair - PAD) * j, PAD)], back.at[k, pl.ds(PAD * j, PAD)],
                back_send.at[j, k], back_recv.at[j, k], to_right,
            )
            for j in range(2)
        )

    def ring_stage(k):
        @pl.when(k < nz - 1)
        def _():
            ring_in(k).wait_recv()

        @pl.when(k < nz - 3)
        def _():
            ring_next(k).start()

        for j in range(2):
            @pl.when(k == nz - 3 + j)
            def _(j=j):
                ring_last(j).start()

        @pl.when(k == nz - 1)
        def _():
            ring_last(0).wait_recv()
            ring_last(1).wait_recv()

    def partner_stage(k):
        slots_to_z(k).wait_recv()
        pick_for_partner(k)

    def gather_stage(k):
        push(xs.at[k], xg.at[k, t], z_send.at[k], z_recv.at[k], to_right).wait_recv()
        start(gather(k))

    def forward_stage(k):
        arrive(gathered(k))
        start(forward(k, left, right))

    def up_stage(k):
        arrive(forward(k, opposite, opposite))
        over_x(k).wait_recv()
        chosen = picked(slot_in[k, pl.ds(xh, 1), :], (CAP * xh).astype(F32), pair)
        theirs = pl.ds(pl.multiple_of((pair - PAD) * (1 - xh), 16), PAD)
        for q in range(ny):
            x1[q] = dot(chosen, xb[k, q]).astype(BF16)
            x1[q, theirs] = x1[q, theirs] + pr[k, q]
        gate_act = up_act = None
        for q in range(ny):
            for x, first, count in (
                (xg[k, q], q * quarter, late), (x1[q], q * quarter + late, quarter - late)
            ):
                g = dot(x, wg[first : first + count, :])
                u = dot(x, wu[first : first + count, :])
                gate_act = g if gate_act is None else gate_act + g
                up_act = u if up_act is None else up_act + u
        hidden[k] = (gate_act / (1.0 + jnp.exp(-gate_act)) * up_act).astype(BF16)
        part = dot(hidden[k], wd[opposite]).astype(BF16)
        s1[0, k] = part[:, :half]
        s1[1, k] = part[:, half:]
        start(relay(k))
        s2[0, k] = dot(hidden[k], wd[right, :, half:]).astype(BF16)
        s2[1, k] = dot(hidden[k], wd[left, :, :half]).astype(BF16)
        start(direct(k))

    def down_stage(k):
        arrive(relay(k))
        h = hidden[k]
        s3[0, k] = (dot(h, wd[right, :, :half]) + r1[0, k].astype(F32)).astype(BF16)
        s3[1, k] = (dot(h, wd[left, :, half:]) + r1[1, k].astype(F32)).astype(BF16)
        start(joined(k))

    def sum_stage(k):
        arrive(direct(k))
        arrive(joined(k))
        part = dot(hidden[k], wd[t])
        ret[k, :, :half] = (part[:, :half] + r3[0, k].astype(F32) + r2[1, k].astype(F32)).astype(BF16)
        ret[k, :, half:] = (part[:, half:] + r2[0, k].astype(F32) + r3[1, k].astype(F32)).astype(BF16)
        start(give_back(k))

    def mix_stage(k):
        arrive(given_back(k))
        y = back[k]
        acc[...] += dot(mix[k, 0], y) + dot(mix[k, 1], y)

    def leave(copies):
        for copy in copies:
            copy.wait_send()

    def drain_stage(k):
        @pl.when(k > 0)
        def _():
            leave((to_z(k), slots_to_z(k)))

        @pl.when((k > 0) & (k < nz - 3))
        def _():
            ring_next(k).wait_send()

        for copies in (
            gather(k), forward(k, left, right), relay(k), direct(k), joined(k), give_back(k),
        ):
            leave(copies)
        over_x(k).wait_send()

    def staged(i, lag, stage, first):
        p = i - lag

        @pl.when((p >= first) & (p < nz))
        def _():
            stage(chunk_at(p))

    def step(i, carry):
        staged(i, -1, forward_stage, 0)
        staged(i, -2, gather_stage, 1)
        staged(i, 0, up_stage, 0)
        staged(i, 1, down_stage, 0)

        @pl.when(i < nz // 2 - 1)
        def _():
            ring_stage(2 * i + 3)

        @pl.when(i < nz // 2 - 2)
        def _():
            ring_stage(2 * i + 4)

        staged(i, -2, partner_stage, 1)
        staged(i, -4, send_stage, 3)

        @pl.when(i == 1)
        def _():
            build_all_mix()

        staged(i, 2, sum_stage, 0)
        staged(i, 4, mix_stage, 0)
        staged(i, 5, drain_stage, 0)
        return carry

    lax.fori_loop(-1, nz + 5, step, 0)
    out_ref[...] = acc[...].astype(out_ref.dtype)

    leave((meta_x, meta_s, tok_x))
    leave(early_out())
    leave(early_pass(left, right))
    leave(ring_first())
    leave((ring_last(0), ring_last(1)))


def on_device(nsec, nz, ny, tokens, expert_ids, gate_values, w_gate, w_up, w_down):
    rows, quarter = tokens.shape[1:]
    width, units = w_gate.shape[2:]
    pair, half = 2 * CAP, quarter // 2
    late = quarter // 2
    early = quarter - late
    dma = pltpu.SemaphoreType.DMA
    vmem = lambda *shape, dtype=BF16: pltpu.VMEM(shape, dtype)
    sides = lambda n: [dma((2, n)), dma((2, n))]
    each = lambda n: [dma((n,)), dma((n,))]
    combined = pl.pallas_call(
        functools.partial(moe_kernel, nsec, nz, ny),
        out_shape=jax.ShapeDtypeStruct((rows, quarter), BF16),
        in_specs=[pl.BlockSpec(memory_space=pltpu.VMEM)] * 3 + [pl.BlockSpec(memory_space=pl.ANY)] * 3,
        out_specs=pl.BlockSpec(memory_space=pltpu.VMEM),
        scratch_shapes=[
            vmem(width, units), vmem(width, units), vmem(ny, units, quarter),
            vmem(3, NAMES, rows, dtype=F32),
            vmem(2, NAMES, rows, dtype=F32),
            vmem(2, rows, late),
            vmem(nz, pair, late),
            vmem(nz, ny, pair, late),
            vmem(nz, 8, rows, dtype=F32), vmem(nz, 8, rows, dtype=F32),
            vmem(nz, ny, rows, early),
            vmem(nz, ny, PAD, early), vmem(nz, ny, PAD, early),
            vmem(ny, pair, early),
            vmem(nz, pair, units),
            vmem(2, nz, pair, half), vmem(2, nz, pair, half),
            vmem(2, nz, pair, half), vmem(2, nz, pair, half),
            vmem(2, nz, pair, half), vmem(2, nz, pair, half),
            vmem(nz, pair, quarter),
            vmem(nz, 2 * PAD, quarter),
            vmem(nz, 2, rows, 2 * PAD),
            vmem(rows, quarter, dtype=F32),
            dma((2 + ny,)), *each(2), dma, dma, *each(nz), *each(nz),
            *sides(1), *sides(1), *each(nz), *each(2), *each(nz),
            *sides(nz), *sides(nz), *sides(nz), *sides(nz), *sides(nz),
            *sides(nz),
        ],
        compiler_params=pltpu.CompilerParams(
            collective_id=0, has_side_effects=True, vmem_limit_bytes=60 * 1024 * 1024
        ),
        cost_estimate=pl.CostEstimate(
            flops=6 * nz * pair * width * units, bytes_accessed=6 * width * units, transcendentals=0
        ),
    )(tokens[0], expert_ids[0].T, gate_values[0].T, w_gate[0, 0], w_up[0, 0], w_down[0, 0])
    return combined[None]


def solution(mesh):
    nsec, nexp, ny = mesh.shape["section"], mesh.shape["expert"], mesh.shape["tensor"]
    in_specs = (
        P("section", "expert", "tensor"),
        P("section", "expert", None),
        P("section", "expert", None),
        P("section", "expert", None, "tensor"),
        P("section", "expert", None, "tensor"),
        P("section", "expert", "tensor", None),
    )
    return jax.shard_map(
        functools.partial(on_device, nsec, nexp // 2, ny),
        mesh=mesh, in_specs=in_specs, out_specs=P("section", "expert", "tensor"), check_vma=False,
    )
```

```python
import functools

import jax
import jax.numpy as jnp
from jax import lax
from jax.experimental import pallas as pl
from jax.experimental.pallas import tpu as pltpu
from jax.sharding import PartitionSpec as P

CAP = 72
PAD = 80
NAMES = 16
BF16 = jnp.bfloat16
F32 = jnp.float32


def iota(shape, dim):
    return lax.broadcasted_iota(jnp.int32, shape, dim)


def dot(a, b):
    return jnp.dot(a, b, preferred_element_type=F32)


def order_of(nz):
    return {2: (0, 1), 4: (0, 1, 3, 2), 8: (0, 1, 4, 5, 6, 7, 3, 2)}[nz]


def moe_kernel(
    nsec, nz, ny,
    tok_ref, ids_ref, gate_ref, wg_hbm, wu_hbm, wd_hbm, out_ref,
    wg, wu, wd, table, slot_t, tok2, xs, xg, slot_out, slot_in, xb, px, pr, x1, hidden,
    s1, r1, s2, r2, s3, r3, ret, back, mix, acc,
    w_sem, meta_send, meta_recv, tok_send, tok_recv, z_send, z_recv, slot_send, slot_recv,
    b1_send, b1_recv, b2_send, b2_recv, ring_send, ring_recv, tail_send, tail_recv, x_send, x_recv,
    g1_send, g1_recv, g2_send, g2_recv, r1_send, r1_recv, r2_send, r2_recv, r3_send, r3_recv,
    back_send, back_recv,
):
    sec, e, t = lax.axis_index("section"), lax.axis_index("expert"), lax.axis_index("tensor")
    z, xh = lax.div(e, 2), lax.rem(e, 2)
    rows, quarter = tok_ref.shape
    half = quarter // 2
    late = xg.shape[3]
    pair = 2 * CAP
    right, left, opposite = lax.rem(t + 1, ny), lax.rem(t + ny - 1, ny), lax.rem(t + 2, ny)
    after, before = lax.rem(sec + 1, nsec), lax.rem(sec + nsec - 1, nsec)

    def away(k):
        return lax.rem(lax.div(k + 1, 2) * (2 * lax.rem(k, 2) - 1) + nz, nz)

    def z_to(k):
        return lax.rem(z + away(k), nz)

    def z_from(k):
        return lax.rem(z - away(k) + nz, nz)

    order = order_of(nz)
    packed = sum(k << (3 * p) for p, k in enumerate(order))

    def chunk_at(p):
        return lax.rem(lax.shift_right_logical(packed, 3 * p), 8)

    loads = [
        pltpu.make_async_copy(wg_hbm, wg, w_sem.at[0]),
        pltpu.make_async_copy(wu_hbm, wu, w_sem.at[1]),
    ] + [
        pltpu.make_async_copy(wd_hbm.at[:, pl.ds(q * quarter, quarter)], wd.at[q], w_sem.at[2 + q])
        for q in range(ny)
    ]
    for load in loads:
        load.start()

    named = iota((NAMES, rows), 0)
    own = jnp.zeros((NAMES, rows), F32)
    for k in range(ids_ref.shape[0]):
        own = own + jnp.where(ids_ref[k : k + 1, :] == named, gate_ref[k : k + 1, :], 0.0)
    table[xh] = own

    barrier = pltpu.get_barrier_semaphore()

    def greet(device):
        pl.semaphore_signal(barrier, inc=1, device_id=device, device_id_type=pl.DeviceIdType.MESH)

    partner = (sec, z * 2 + 1 - xh, t)
    to_right, to_left = (sec, e, right), (sec, e, left)
    greet(to_right)
    greet(to_left)
    greet(partner)
    for k in range(1, nz):
        greet((sec, z_from(k) * 2 + xh, t))
    for other in range(2 * nz):
        greet((before, other, t))
    pl.semaphore_wait(barrier, (nz - 1) + 3 + 2 * nz)

    def push(src, dst, send, recv, device):
        return pltpu.make_async_remote_copy(
            src_ref=src, dst_ref=dst, send_sem=send, recv_sem=recv,
            device_id=device, device_id_type=pl.DeviceIdType.MESH,
        )

    def both_ways(a, b, send, recv, k):
        return (
            push(a[0], a[1], send.at[0, k], recv.at[0, k], to_right),
            push(b[0], b[1], send.at[1, k], recv.at[1, k], to_left),
        )

    def start(copies):
        for copy in copies:
            copy.start()

    def arrive(copies):
        for copy in copies:
            copy.wait_recv()

    def early_out():
        a = (tok_ref.at[:, pl.ds(late, quarter - late)], xb.at[0, t])
        return both_ways(a, a, b1_send, b1_recv, 0)

    def early_in():
        a, b = xb.at[0, left], xb.at[0, right]
        return both_ways((a, a), (b, b), b1_send, b1_recv, 0)

    def early_pass(from_left, from_right):
        a = xb.at[0, from_left, pl.ds(0, rows // 2)]
        b = xb.at[0, from_right, pl.ds(rows // 2, rows // 2)]
        return both_ways((a, a), (b, b), b2_send, b2_recv, 0)

    meta_x = push(table.at[xh], table.at[xh], meta_send.at[0], meta_recv.at[0], partner)
    meta_s = push(table.at[xh], table.at[2], meta_send.at[1], meta_recv.at[1], (after, e, t))
    late_part = tok_ref.at[:, pl.ds(0, late)]
    tok_x = push(late_part, tok2.at[xh], tok_send, tok_recv, partner)
    meta_x.start()
    tok_x.start()
    start(early_out())
    meta_s.start()
    tok2[xh] = tok_ref[:, :late]
    xb[0, t] = tok_ref[:, late:]

    earlier = (iota((rows, rows), 0) < iota((rows, rows), 1)).astype(BF16)

    def slots_by_expert(gates):
        names = (gates > 0).astype(F32)
        return jnp.where(names > 0, dot(names.astype(BF16), earlier), -1000.0)

    slot_t[xh] = slots_by_expert(own)
    push(table.at[1 - xh], table.at[1 - xh], meta_send.at[0], meta_recv.at[0], partner).wait_recv()
    slot_t[1 - xh] = slots_by_expert(table[1 - xh])
    arrive(early_in())
    start(early_pass(left, right))

    def to_z(k):
        return push(xs.at[k], xg.at[k, t], z_send.at[k], z_recv.at[k], (sec, z_to(k) * 2 + xh, t))

    def slots_to_z(k):
        return push(
            slot_out.at[k], slot_in.at[k], slot_send.at[k], slot_recv.at[k],
            (sec, z_to(k) * 2 + xh, t),
        )

    def picked(slots, shift, count):
        return (slots + shift == iota((count, rows), 0).astype(F32)).astype(BF16)

    def pick(k):
        expert = z_to(k) * 2 + xh
        chosen = [picked(slot_t[j, pl.ds(expert, 1), :], float(CAP * j), pair) for j in range(2)]
        return (dot(chosen[0], tok2[0]) + dot(chosen[1], tok2[1])).astype(BF16)

    def gather(k):
        a = xg.at[k, t]
        return both_ways((a, a), (a, a), g1_send, g1_recv, k)

    def gathered(k):
        a, b = xg.at[k, left], xg.at[k, right]
        return both_ways((a, a), (b, b), g1_send, g1_recv, k)

    def forward(k, from_left, from_right):
        a = xg.at[k, from_left, :, pl.ds(0, late // 2)]
        b = xg.at[k, from_right, :, pl.ds(late // 2, late // 2)]
        return both_ways((a, a), (b, b), g2_send, g2_recv, k)

    push(late_part, tok2.at[1 - xh], tok_send, tok_recv, partner).wait_recv()
    xg[0, t] = pick(0)
    start(gather(0))

    def ring_next(k):
        dz = 2 * lax.rem(k, 2) - 1
        device = (sec, lax.rem(z + dz + nz, nz) * 2 + xh, t)
        return push(xb.at[k], xb.at[k + 2], ring_send.at[k], ring_recv.at[k + 2], device)

    up_z, down_z = (sec, lax.rem(z + 1, nz) * 2 + xh, t), (sec, lax.rem(z + nz - 1, nz) * 2 + xh, t)

    def ring_first():
        return (
            push(xb.at[0], xb.at[1], ring_send.at[nz - 2], ring_recv.at[1], up_z),
            push(xb.at[0], xb.at[2], ring_send.at[nz - 1], ring_recv.at[2], down_z),
        )

    def ring_in(k):
        return push(xb.at[0], xb.at[k], ring_send.at[0], ring_recv.at[k], up_z)

    def ring_last(j):
        part = pl.ds(j * (ny // 2), ny // 2)
        return push(
            xb.at[nz - 3 + j, part], xb.at[nz - 1, part], tail_send.at[j], tail_recv.at[j],
            (up_z, down_z)[j],
        )

    def over_x(k):
        return push(px.at[k], pr.at[k], x_send.at[k], x_recv.at[k], partner)

    def pick_for_partner(k):
        chosen = picked(slot_in[k, pl.ds(1 - xh, 1), :], ((PAD - CAP) * xh).astype(F32), PAD)
        for q in range(ny):
            px[k, q] = dot(chosen, xb[k, q]).astype(BF16)
        over_x(k).start()

    slot_in[0, 0:1, :] = slot_t[xh, pl.ds(z * 2, 1), :]
    slot_in[0, 1:2, :] = slot_t[xh, pl.ds(z * 2 + 1, 1), :]
    def send_stage(k):
        xs[k] = pick(k)
        to_z(k).start()

    for p in (1, 2):
        if p < nz:
            send_stage(jnp.int32(order[p]))

    arrive(early_pass(opposite, opposite))
    start(ring_first())

    def send_slots(k, carry):
        for j in range(2):
            slot_out[k, j : j + 1, :] = slot_t[xh, pl.ds(z_to(k) * 2 + j, 1), :]
        slots_to_z(k).start()
        return carry

    lax.fori_loop(1, nz, send_slots, 0)
    pick_for_partner(0)

    for load in loads:
        load.wait()

    def build_all_mix():
        push(table.at[2], table.at[2], meta_send.at[1], meta_recv.at[1], (after, e, t)).wait_recv()
        filler = jnp.zeros((128 - NAMES, rows), F32)
        gates = jnp.transpose(jnp.concatenate([table[2], filler], axis=0))
        slots = jnp.transpose(jnp.concatenate([slots_by_expert(table[2]), filler], axis=0))
        lanes = iota((rows, 128), 1)
        place = iota((rows, 2 * PAD), 1).astype(F32)

        def build_mix(k, carry):
            total = jnp.zeros((rows, 2 * PAD), F32)
            for j in range(2):
                here = lanes == z_to(k) * 2 + j
                gate = jnp.sum(jnp.where(here, gates, 0.0), axis=1, keepdims=True)
                slot = jnp.sum(jnp.where(here, slots, 0.0), axis=1, keepdims=True)
                at = slot + ((PAD - CAP) * xh).astype(F32) + float(PAD * j)
                total = total + jnp.where(place == at, gate, 0.0)
            high = total.astype(BF16)
            mix[k, 0] = high
            mix[k, 1] = (total - high.astype(F32)).astype(BF16)
            return carry

        lax.fori_loop(0, nz, build_mix, 0)
        acc[...] = jnp.zeros_like(acc)

    def relay(k):
        return both_ways((s1.at[0, k], r1.at[0, k]), (s1.at[1, k], r1.at[1, k]), r1_send, r1_recv, k)

    def direct(k):
        return both_ways((s2.at[0, k], r2.at[0, k]), (s2.at[1, k], r2.at[1, k]), r2_send, r2_recv, k)

    def joined(k):
        return both_ways((s3.at[0, k], r3.at[0, k]), (s3.at[1, k], r3.at[1, k]), r3_send, r3_recv, k)

    def give_back(k):
        return tuple(
            push(
                ret.at[k, pl.ds((pair - PAD) * j, PAD)], back.at[k, pl.ds(PAD * xh, PAD)],
                back_send.at[j, k], back_recv.at[xh, k], (after, z_from(k) * 2 + j, t),
            )
            for j in range(2)
        )

    def given_back(k):
        return tuple(
            push(
                ret.at[k, pl.ds((pair - PAD) * j, PAD)], back.at[k, pl.ds(PAD * j, PAD)],
                back_send.at[j, k], back_recv.at[j, k], to_right,
            )
            for j in range(2)
        )

    def ring_stage(k):
        @pl.when(k < nz - 1)
        def _():
            ring_in(k).wait_recv()

        @pl.when(k < nz - 3)
        def _():
            ring_next(k).start()

        for j in range(2):
            @pl.when(k == nz - 3 + j)
            def _(j=j):
                ring_last(j).start()

        @pl.when(k == nz - 1)
        def _():
            ring_last(0).wait_recv()
            ring_last(1).wait_recv()

    def partner_stage(k):
        slots_to_z(k).wait_recv()
        pick_for_partner(k)

    def gather_stage(k):
        push(xs.at[k], xg.at[k, t], z_send.at[k], z_recv.at[k], to_right).wait_recv()
        start(gather(k))

    def forward_stage(k):
        arrive(gathered(k))
        start(forward(k, left, right))

    def up_stage(k):
        arrive(forward(k, opposite, opposite))
        over_x(k).wait_recv()
        chosen = picked(slot_in[k, pl.ds(xh, 1), :], (CAP * xh).astype(F32), pair)
        theirs = pl.ds(pl.multiple_of((pair - PAD) * (1 - xh), 16), PAD)
        for q in range(ny):
            x1[q] = dot(chosen, xb[k, q]).astype(BF16)
            x1[q, theirs] = x1[q, theirs] + pr[k, q]
        gate_act = up_act = None
        for q in range(ny):
            for x, first, count in (
                (xg[k, q], q * quarter, late), (x1[q], q * quarter + late, quarter - late)
            ):
                g = dot(x, wg[first : first + count, :])
                u = dot(x, wu[first : first + count, :])
                gate_act = g if gate_act is None else gate_act + g
                up_act = u if up_act is None else up_act + u
        hidden[k] = (gate_act / (1.0 + jnp.exp(-gate_act)) * up_act).astype(BF16)
        part = dot(hidden[k], wd[opposite]).astype(BF16)
        s1[0, k] = part[:, :half]
        s1[1, k] = part[:, half:]
        start(relay(k))
        s2[0, k] = dot(hidden[k], wd[right, :, half:]).astype(BF16)
        s2[1, k] = dot(hidden[k], wd[left, :, :half]).astype(BF16)
        start(direct(k))

    def down_stage(k):
        arrive(relay(k))
        h = hidden[k]
        s3[0, k] = (dot(h, wd[right, :, :half]) + r1[0, k].astype(F32)).astype(BF16)
        s3[1, k] = (dot(h, wd[left, :, half:]) + r1[1, k].astype(F32)).astype(BF16)
        start(joined(k))

    def sum_stage(k):
        arrive(direct(k))
        arrive(joined(k))
        part = dot(hidden[k], wd[t])
        ret[k, :, :half] = (part[:, :half] + r3[0, k].astype(F32) + r2[1, k].astype(F32)).astype(BF16)
        ret[k, :, half:] = (part[:, half:] + r2[0, k].astype(F32) + r3[1, k].astype(F32)).astype(BF16)
        start(give_back(k))

    def mix_stage(k):
        arrive(given_back(k))
        y = back[k]
        acc[...] += dot(mix[k, 0], y) + dot(mix[k, 1], y)

    def leave(copies):
        for copy in copies:
            copy.wait_send()

    def drain_stage(k):
        @pl.when(k > 0)
        def _():
            leave((to_z(k), slots_to_z(k)))

        @pl.when((k > 0) & (k < nz - 3))
        def _():
            ring_next(k).wait_send()

        for copies in (
            gather(k), forward(k, left, right), relay(k), direct(k), joined(k), give_back(k),
        ):
            leave(copies)
        over_x(k).wait_send()

    def staged(i, lag, stage, first):
        p = i - lag

        @pl.when((p >= first) & (p < nz))
        def _():
            stage(chunk_at(p))

    def step(i, carry):
        staged(i, 2, sum_stage, 0)
        staged(i, 1, down_stage, 0)
        staged(i, -1, forward_stage, 0)
        staged(i, 0, up_stage, 0)
        staged(i, -2, gather_stage, 1)

        @pl.when(i < nz // 2 - 1)
        def _():
            ring_stage(2 * i + 3)

        @pl.when(i < nz // 2 - 2)
        def _():
            ring_stage(2 * i + 4)

        staged(i, -2, partner_stage, 1)
        staged(i, -4, send_stage, 3)

        @pl.when(i == 1)
        def _():
            build_all_mix()

        staged(i, 4, mix_stage, 0)
        staged(i, 5, drain_stage, 0)
        return carry

    lax.fori_loop(-1, nz + 5, step, 0)
    out_ref[...] = acc[...].astype(out_ref.dtype)

    leave((meta_x, meta_s, tok_x))
    leave(early_out())
    leave(early_pass(left, right))
    leave(ring_first())
    leave((ring_last(0), ring_last(1)))


def on_device(nsec, nz, ny, tokens, expert_ids, gate_values, w_gate, w_up, w_down):
    rows, quarter = tokens.shape[1:]
    width, units = w_gate.shape[2:]
    pair, half = 2 * CAP, quarter // 2
    late = quarter // 2
    early = quarter - late
    dma = pltpu.SemaphoreType.DMA
    vmem = lambda *shape, dtype=BF16: pltpu.VMEM(shape, dtype)
    sides = lambda n: [dma((2, n)), dma((2, n))]
    each = lambda n: [dma((n,)), dma((n,))]
    combined = pl.pallas_call(
        functools.partial(moe_kernel, nsec, nz, ny),
        out_shape=jax.ShapeDtypeStruct((rows, quarter), BF16),
        in_specs=[pl.BlockSpec(memory_space=pltpu.VMEM)] * 3 + [pl.BlockSpec(memory_space=pl.ANY)] * 3,
        out_specs=pl.BlockSpec(memory_space=pltpu.VMEM),
        scratch_shapes=[
            vmem(width, units), vmem(width, units), vmem(ny, units, quarter),
            vmem(3, NAMES, rows, dtype=F32),
            vmem(2, NAMES, rows, dtype=F32),
            vmem(2, rows, late),
            vmem(nz, pair, late),
            vmem(nz, ny, pair, late),
            vmem(nz, 8, rows, dtype=F32), vmem(nz, 8, rows, dtype=F32),
            vmem(nz, ny, rows, early),
            vmem(nz, ny, PAD, early), vmem(nz, ny, PAD, early),
            vmem(ny, pair, early),
            vmem(nz, pair, units),
            vmem(2, nz, pair, half), vmem(2, nz, pair, half),
            vmem(2, nz, pair, half), vmem(2, nz, pair, half),
            vmem(2, nz, pair, half), vmem(2, nz, pair, half),
            vmem(nz, pair, quarter),
            vmem(nz, 2 * PAD, quarter),
            vmem(nz, 2, rows, 2 * PAD),
            vmem(rows, quarter, dtype=F32),
            dma((2 + ny,)), *each(2), dma, dma, *each(nz), *each(nz),
            *sides(1), *sides(1), *each(nz), *each(2), *each(nz),
            *sides(nz), *sides(nz), *sides(nz), *sides(nz), *sides(nz),
            *sides(nz),
        ],
        compiler_params=pltpu.CompilerParams(
            collective_id=0, has_side_effects=True, vmem_limit_bytes=60 * 1024 * 1024
        ),
        cost_estimate=pl.CostEstimate(
            flops=6 * nz * pair * width * units, bytes_accessed=6 * width * units, transcendentals=0
        ),
    )(tokens[0], expert_ids[0].T, gate_values[0].T, w_gate[0, 0], w_up[0, 0], w_down[0, 0])
    return combined[None]


def solution(mesh):
    nsec, nexp, ny = mesh.shape["section"], mesh.shape["expert"], mesh.shape["tensor"]
    in_specs = (
        P("section", "expert", "tensor"),
        P("section", "expert", None),
        P("section", "expert", None),
        P("section", "expert", None, "tensor"),
        P("section", "expert", None, "tensor"),
        P("section", "expert", "tensor", None),
    )
    return jax.shard_map(
        functools.partial(on_device, nsec, nexp // 2, ny),
        mesh=mesh, in_specs=in_specs, out_specs=P("section", "expert", "tensor"), check_vma=False,
    )
```

```python
import functools

import jax
import jax.numpy as jnp
from jax import lax
from jax.experimental import pallas as pl
from jax.experimental.pallas import tpu as pltpu
from jax.sharding import PartitionSpec as P

CAP = 72
PAD = 80
NAMES = 16
BF16 = jnp.bfloat16
F32 = jnp.float32


def iota(shape, dim):
    return lax.broadcasted_iota(jnp.int32, shape, dim)


def dot(a, b):
    return jnp.dot(a, b, preferred_element_type=F32)


def order_of(nz):
    return {2: (0, 1), 4: (0, 1, 3, 2), 8: (0, 1, 4, 5, 6, 7, 3, 2)}[nz]


def moe_kernel(
    nsec, nz, ny,
    tok_ref, ids_ref, gate_ref, wg_hbm, wu_hbm, wd_hbm, out_ref,
    wg, wu, wd, table, slot_t, tok2, xs, xg, slot_out, slot_in, xb, px, pr, x1, hidden,
    s1, r1, s2, r2, s3, r3, ret, back, mix, acc,
    w_sem, meta_send, meta_recv, tok_send, tok_recv, z_send, z_recv, slot_send, slot_recv,
    b1_send, b1_recv, b2_send, b2_recv, ring_send, ring_recv, tail_send, tail_recv, x_send, x_recv,
    g1_send, g1_recv, g2_send, g2_recv, r1_send, r1_recv, r2_send, r2_recv, r3_send, r3_recv,
    back_send, back_recv,
):
    sec, e, t = lax.axis_index("section"), lax.axis_index("expert"), lax.axis_index("tensor")
    z, xh = lax.div(e, 2), lax.rem(e, 2)
    rows, quarter = tok_ref.shape
    half = quarter // 2
    late = xg.shape[3]
    pair = 2 * CAP
    right, left, opposite = lax.rem(t + 1, ny), lax.rem(t + ny - 1, ny), lax.rem(t + 2, ny)
    after, before = lax.rem(sec + 1, nsec), lax.rem(sec + nsec - 1, nsec)

    def away(k):
        return lax.rem(lax.div(k + 1, 2) * (2 * lax.rem(k, 2) - 1) + nz, nz)

    def z_to(k):
        return lax.rem(z + away(k), nz)

    def z_from(k):
        return lax.rem(z - away(k) + nz, nz)

    order = order_of(nz)
    packed = sum(k << (3 * p) for p, k in enumerate(order))

    def chunk_at(p):
        return lax.rem(lax.shift_right_logical(packed, 3 * p), 8)

    loads = [
        pltpu.make_async_copy(wg_hbm, wg, w_sem.at[0]),
        pltpu.make_async_copy(wu_hbm, wu, w_sem.at[1]),
    ] + [
        pltpu.make_async_copy(wd_hbm.at[:, pl.ds(q * quarter, quarter)], wd.at[q], w_sem.at[2 + q])
        for q in range(ny)
    ]
    for load in loads:
        load.start()

    named = iota((NAMES, rows), 0)
    own = jnp.zeros((NAMES, rows), F32)
    for k in range(ids_ref.shape[0]):
        own = own + jnp.where(ids_ref[k : k + 1, :] == named, gate_ref[k : k + 1, :], 0.0)
    table[xh] = own

    barrier = pltpu.get_barrier_semaphore()

    def greet(device):
        pl.semaphore_signal(barrier, inc=1, device_id=device, device_id_type=pl.DeviceIdType.MESH)

    partner = (sec, z * 2 + 1 - xh, t)
    to_right, to_left = (sec, e, right), (sec, e, left)
    greet(to_right)
    greet(to_left)
    greet(partner)
    for k in range(1, nz):
        greet((sec, z_from(k) * 2 + xh, t))
    for other in range(2 * nz):
        greet((before, other, t))
    pl.semaphore_wait(barrier, (nz - 1) + 3 + 2 * nz)

    def push(src, dst, send, recv, device):
        return pltpu.make_async_remote_copy(
            src_ref=src, dst_ref=dst, send_sem=send, recv_sem=recv,
            device_id=device, device_id_type=pl.DeviceIdType.MESH,
        )

    def both_ways(a, b, send, recv, k):
        return (
            push(a[0], a[1], send.at[0, k], recv.at[0, k], to_right),
            push(b[0], b[1], send.at[1, k], recv.at[1, k], to_left),
        )

    def start(copies):
        for copy in copies:
            copy.start()

    def arrive(copies):
        for copy in copies:
            copy.wait_recv()

    def early_out():
        a = (tok_ref.at[:, pl.ds(late, quarter - late)], xb.at[0, t])
        return both_ways(a, a, b1_send, b1_recv, 0)

    def early_in():
        a, b = xb.at[0, left], xb.at[0, right]
        return both_ways((a, a), (b, b), b1_send, b1_recv, 0)

    def early_pass(from_left, from_right):
        a = xb.at[0, from_left, pl.ds(0, rows // 2)]
        b = xb.at[0, from_right, pl.ds(rows // 2, rows // 2)]
        return both_ways((a, a), (b, b), b2_send, b2_recv, 0)

    meta_x = push(table.at[xh], table.at[xh], meta_send.at[0], meta_recv.at[0], partner)
    meta_s = push(table.at[xh], table.at[2], meta_send.at[1], meta_recv.at[1], (after, e, t))
    late_part = tok_ref.at[:, pl.ds(0, late)]
    tok_x = push(late_part, tok2.at[xh], tok_send, tok_recv, partner)
    meta_x.start()
    tok_x.start()
    start(early_out())
    meta_s.start()
    tok2[xh] = tok_ref[:, :late]
    xb[0, t] = tok_ref[:, late:]

    earlier = (iota((rows, rows), 0) < iota((rows, rows), 1)).astype(BF16)

    def slots_by_expert(gates):
        names = (gates > 0).astype(F32)
        return jnp.where(names > 0, dot(names.astype(BF16), earlier), -1000.0)

    slot_t[xh] = slots_by_expert(own)
    push(table.at[1 - xh], table.at[1 - xh], meta_send.at[0], meta_recv.at[0], partner).wait_recv()
    slot_t[1 - xh] = slots_by_expert(table[1 - xh])
    arrive(early_in())
    start(early_pass(left, right))

    def to_z(k):
        return push(xs.at[k], xg.at[k, t], z_send.at[k], z_recv.at[k], (sec, z_to(k) * 2 + xh, t))

    def slots_to_z(k):
        return push(
            slot_out.at[k], slot_in.at[k], slot_send.at[k], slot_recv.at[k],
            (sec, z_to(k) * 2 + xh, t),
        )

    def picked(slots, shift, count):
        return (slots + shift == iota((count, rows), 0).astype(F32)).astype(BF16)

    def pick(k):
        expert = z_to(k) * 2 + xh
        chosen = [picked(slot_t[j, pl.ds(expert, 1), :], float(CAP * j), pair) for j in range(2)]
        return (dot(chosen[0], tok2[0]) + dot(chosen[1], tok2[1])).astype(BF16)

    def gather(k):
        a = xg.at[k, t]
        return both_ways((a, a), (a, a), g1_send, g1_recv, k)

    def gathered(k):
        a, b = xg.at[k, left], xg.at[k, right]
        return both_ways((a, a), (b, b), g1_send, g1_recv, k)

    def forward(k, from_left, from_right):
        a = xg.at[k, from_left, pl.ds(0, PAD)]
        b = xg.at[k, from_right, pl.ds(PAD, pair - PAD)]
        return both_ways((a, a), (b, b), g2_send, g2_recv, k)

    push(late_part, tok2.at[1 - xh], tok_send, tok_recv, partner).wait_recv()
    xg[0, t] = pick(0)
    start(gather(0))

    def ring_next(k):
        dz = 2 * lax.rem(k, 2) - 1
        device = (sec, lax.rem(z + dz + nz, nz) * 2 + xh, t)
        return push(xb.at[k], xb.at[k + 2], ring_send.at[k], ring_recv.at[k + 2], device)

    up_z, down_z = (sec, lax.rem(z + 1, nz) * 2 + xh, t), (sec, lax.rem(z + nz - 1, nz) * 2 + xh, t)

    def ring_first():
        return (
            push(xb.at[0], xb.at[1], ring_send.at[nz - 2], ring_recv.at[1], up_z),
            push(xb.at[0], xb.at[2], ring_send.at[nz - 1], ring_recv.at[2], down_z),
        )

    def ring_in(k):
        return push(xb.at[0], xb.at[k], ring_send.at[0], ring_recv.at[k], up_z)

    def ring_last(j):
        part = pl.ds(j * (ny // 2), ny // 2)
        return push(
            xb.at[nz - 3 + j, part], xb.at[nz - 1, part], tail_send.at[j], tail_recv.at[j],
            (up_z, down_z)[j],
        )

    def over_x(k):
        return push(px.at[k], pr.at[k], x_send.at[k], x_recv.at[k], partner)

    def pick_for_partner(k):
        chosen = picked(slot_in[k, pl.ds(1 - xh, 1), :], ((PAD - CAP) * xh).astype(F32), PAD)
        for q in range(ny):
            px[k, q] = dot(chosen, xb[k, q]).astype(BF16)
        over_x(k).start()

    slot_in[0, 0:1, :] = slot_t[xh, pl.ds(z * 2, 1), :]
    slot_in[0, 1:2, :] = slot_t[xh, pl.ds(z * 2 + 1, 1), :]
    def send_stage(k):
        xs[k] = pick(k)
        to_z(k).start()

    for p in (1, 2):
        if p < nz:
            send_stage(jnp.int32(order[p]))

    arrive(early_pass(opposite, opposite))
    start(ring_first())

    def send_slots(k, carry):
        for j in range(2):
            slot_out[k, j : j + 1, :] = slot_t[xh, pl.ds(z_to(k) * 2 + j, 1), :]
        slots_to_z(k).start()
        return carry

    lax.fori_loop(1, nz, send_slots, 0)
    pick_for_partner(0)

    for load in loads:
        load.wait()

    def build_all_mix():
        push(table.at[2], table.at[2], meta_send.at[1], meta_recv.at[1], (after, e, t)).wait_recv()
        filler = jnp.zeros((128 - NAMES, rows), F32)
        gates = jnp.transpose(jnp.concatenate([table[2], filler], axis=0))
        slots = jnp.transpose(jnp.concatenate([slots_by_expert(table[2]), filler], axis=0))
        lanes = iota((rows, 128), 1)
        place = iota((rows, 2 * PAD), 1).astype(F32)

        def build_mix(k, carry):
            total = jnp.zeros((rows, 2 * PAD), F32)
            for j in range(2):
                here = lanes == z_to(k) * 2 + j
                gate = jnp.sum(jnp.where(here, gates, 0.0), axis=1, keepdims=True)
                slot = jnp.sum(jnp.where(here, slots, 0.0), axis=1, keepdims=True)
                at = slot + ((PAD - CAP) * xh).astype(F32) + float(PAD * j)
                total = total + jnp.where(place == at, gate, 0.0)
            high = total.astype(BF16)
            mix[k, 0] = high
            mix[k, 1] = (total - high.astype(F32)).astype(BF16)
            return carry

        lax.fori_loop(0, nz, build_mix, 0)
        acc[...] = jnp.zeros_like(acc)

    def relay(k):
        return both_ways((s1.at[0, k], r1.at[0, k]), (s1.at[1, k], r1.at[1, k]), r1_send, r1_recv, k)

    def direct(k):
        return both_ways((s2.at[0, k], r2.at[0, k]), (s2.at[1, k], r2.at[1, k]), r2_send, r2_recv, k)

    def joined(k):
        return both_ways((s3.at[0, k], r3.at[0, k]), (s3.at[1, k], r3.at[1, k]), r3_send, r3_recv, k)

    def give_back(k):
        return tuple(
            push(
                ret.at[k, pl.ds((pair - PAD) * j, PAD)], back.at[k, pl.ds(PAD * xh, PAD)],
                back_send.at[j, k], back_recv.at[xh, k], (after, z_from(k) * 2 + j, t),
            )
            for j in range(2)
        )

    def given_back(k):
        return tuple(
            push(
                ret.at[k, pl.ds((pair - PAD) * j, PAD)], back.at[k, pl.ds(PAD * j, PAD)],
                back_send.at[j, k], back_recv.at[j, k], to_right,
            )
            for j in range(2)
        )

    def ring_stage(k):
        @pl.when(k < nz - 1)
        def _():
            ring_in(k).wait_recv()

        @pl.when(k < nz - 3)
        def _():
            ring_next(k).start()

        for j in range(2):
            @pl.when(k == nz - 3 + j)
            def _(j=j):
                ring_last(j).start()

        @pl.when(k == nz - 1)
        def _():
            ring_last(0).wait_recv()
            ring_last(1).wait_recv()

    def partner_stage(k):
        slots_to_z(k).wait_recv()
        pick_for_partner(k)

    def gather_stage(k):
        push(xs.at[k], xg.at[k, t], z_send.at[k], z_recv.at[k], to_right).wait_recv()
        start(gather(k))

    def forward_stage(k):
        arrive(gathered(k))
        start(forward(k, left, right))

    def up_stage(k):
        arrive(forward(k, opposite, opposite))
        over_x(k).wait_recv()
        chosen = picked(slot_in[k, pl.ds(xh, 1), :], (CAP * xh).astype(F32), pair)
        theirs = pl.ds(pl.multiple_of((pair - PAD) * (1 - xh), 16), PAD)
        for q in range(ny):
            x1[q] = dot(chosen, xb[k, q]).astype(BF16)
            x1[q, theirs] = x1[q, theirs] + pr[k, q]
        gate_act = up_act = None
        for q in range(ny):
            for x, first, count in (
                (xg[k, q], q * quarter, late), (x1[q], q * quarter + late, quarter - late)
            ):
                g = dot(x, wg[first : first + count, :])
                u = dot(x, wu[first : first + count, :])
                gate_act = g if gate_act is None else gate_act + g
                up_act = u if up_act is None else up_act + u
        hidden[k] = (gate_act / (1.0 + jnp.exp(-gate_act)) * up_act).astype(BF16)
        part = dot(hidden[k], wd[opposite]).astype(BF16)
        s1[0, k] = part[:, :half]
        s1[1, k] = part[:, half:]
        start(relay(k))
        s2[0, k] = dot(hidden[k], wd[right, :, half:]).astype(BF16)
        s2[1, k] = dot(hidden[k], wd[left, :, :half]).astype(BF16)
        start(direct(k))

    def down_stage(k):
        arrive(relay(k))
        h = hidden[k]
        s3[0, k] = (dot(h, wd[right, :, :half]) + r1[0, k].astype(F32)).astype(BF16)
        s3[1, k] = (dot(h, wd[left, :, half:]) + r1[1, k].astype(F32)).astype(BF16)
        start(joined(k))

    def sum_stage(k):
        arrive(direct(k))
        arrive(joined(k))
        part = dot(hidden[k], wd[t])
        ret[k, :, :half] = (part[:, :half] + r3[0, k].astype(F32) + r2[1, k].astype(F32)).astype(BF16)
        ret[k, :, half:] = (part[:, half:] + r2[0, k].astype(F32) + r3[1, k].astype(F32)).astype(BF16)
        start(give_back(k))

    def mix_stage(k):
        arrive(given_back(k))
        y = back[k]
        acc[...] += dot(mix[k, 0], y) + dot(mix[k, 1], y)

    def leave(copies):
        for copy in copies:
            copy.wait_send()

    def drain_stage(k):
        @pl.when(k > 0)
        def _():
            leave((to_z(k), slots_to_z(k)))

        @pl.when((k > 0) & (k < nz - 3))
        def _():
            ring_next(k).wait_send()

        for copies in (
            gather(k), forward(k, left, right), relay(k), direct(k), joined(k), give_back(k),
        ):
            leave(copies)
        over_x(k).wait_send()

    def staged(i, lag, stage, first):
        p = i - lag

        @pl.when((p >= first) & (p < nz))
        def _():
            stage(chunk_at(p))

    def step(i, carry):
        staged(i, 2, sum_stage, 0)
        staged(i, 1, down_stage, 0)
        staged(i, -1, forward_stage, 0)
        staged(i, 0, up_stage, 0)

        @pl.when((i >= 0) & (i < nz // 2))
        def _():
            ring_stage(2 * i + 1)

        @pl.when((i >= 0) & (i < nz // 2 - 1))
        def _():
            ring_stage(2 * i + 2)

        staged(i, -1, partner_stage, 1)
        staged(i, -2, gather_stage, 1)
        staged(i, -4, send_stage, 3)

        @pl.when(i == 1)
        def _():
            build_all_mix()

        staged(i, 4, mix_stage, 0)
        staged(i, 5, drain_stage, 0)
        return carry

    lax.fori_loop(-1, nz + 5, step, 0)
    out_ref[...] = acc[...].astype(out_ref.dtype)

    leave((meta_x, meta_s, tok_x))
    leave(early_out())
    leave(early_pass(left, right))
    leave(ring_first())
    leave((ring_last(0), ring_last(1)))


def on_device(nsec, nz, ny, tokens, expert_ids, gate_values, w_gate, w_up, w_down):
    rows, quarter = tokens.shape[1:]
    width, units = w_gate.shape[2:]
    pair, half = 2 * CAP, quarter // 2
    late = 5 * quarter // 8
    early = quarter - late
    dma = pltpu.SemaphoreType.DMA
    vmem = lambda *shape, dtype=BF16: pltpu.VMEM(shape, dtype)
    sides = lambda n: [dma((2, n)), dma((2, n))]
    each = lambda n: [dma((n,)), dma((n,))]
    combined = pl.pallas_call(
        functools.partial(moe_kernel, nsec, nz, ny),
        out_shape=jax.ShapeDtypeStruct((rows, quarter), BF16),
        in_specs=[pl.BlockSpec(memory_space=pltpu.VMEM)] * 3 + [pl.BlockSpec(memory_space=pl.ANY)] * 3,
        out_specs=pl.BlockSpec(memory_space=pltpu.VMEM),
        scratch_shapes=[
            vmem(width, units), vmem(width, units), vmem(ny, units, quarter),
            vmem(3, NAMES, rows, dtype=F32),
            vmem(2, NAMES, rows, dtype=F32),
            vmem(2, rows, late),
            vmem(nz, pair, late),
            vmem(nz, ny, pair, late),
            vmem(nz, 8, rows, dtype=F32), vmem(nz, 8, rows, dtype=F32),
            vmem(nz, ny, rows, early),
            vmem(nz, ny, PAD, early), vmem(nz, ny, PAD, early),
            vmem(ny, pair, early),
            vmem(nz, pair, units),
            vmem(2, nz, pair, half), vmem(2, nz, pair, half),
            vmem(2, nz, pair, half), vmem(2, nz, pair, half),
            vmem(2, nz, pair, half), vmem(2, nz, pair, half),
            vmem(nz, pair, quarter),
            vmem(nz, 2 * PAD, quarter),
            vmem(nz, 2, rows, 2 * PAD),
            vmem(rows, quarter, dtype=F32),
            dma((2 + ny,)), *each(2), dma, dma, *each(nz), *each(nz),
            *sides(1), *sides(1), *each(nz), *each(2), *each(nz),
            *sides(nz), *sides(nz), *sides(nz), *sides(nz), *sides(nz),
            *sides(nz),
        ],
        compiler_params=pltpu.CompilerParams(
            collective_id=0, has_side_effects=True, vmem_limit_bytes=60 * 1024 * 1024
        ),
        cost_estimate=pl.CostEstimate(
            flops=6 * nz * pair * width * units, bytes_accessed=6 * width * units, transcendentals=0
        ),
    )(tokens[0], expert_ids[0].T, gate_values[0].T, w_gate[0, 0], w_up[0, 0], w_down[0, 0])
    return combined[None]


def solution(mesh):
    nsec, nexp, ny = mesh.shape["section"], mesh.shape["expert"], mesh.shape["tensor"]
    in_specs = (
        P("section", "expert", "tensor"),
        P("section", "expert", None),
        P("section", "expert", None),
        P("section", "expert", None, "tensor"),
        P("section", "expert", None, "tensor"),
        P("section", "expert", "tensor", None),
    )
    return jax.shard_map(
        functools.partial(on_device, nsec, nexp // 2, ny),
        mesh=mesh, in_specs=in_specs, out_specs=P("section", "expert", "tensor"), check_vma=False,
    )
```

```python
import functools

import jax
import jax.numpy as jnp
from jax import lax
from jax.experimental import pallas as pl
from jax.experimental.pallas import tpu as pltpu
from jax.sharding import PartitionSpec as P

CAP = 72
PAD = 80
NAMES = 16
BF16 = jnp.bfloat16
F32 = jnp.float32


def iota(shape, dim):
    return lax.broadcasted_iota(jnp.int32, shape, dim)


def dot(a, b):
    return jnp.dot(a, b, preferred_element_type=F32)


def order_of(nz):
    return {2: (0, 1), 4: (0, 1, 3, 2), 8: (0, 1, 4, 5, 6, 7, 3, 2)}[nz]


def moe_kernel(
    nsec, nz, ny,
    tok_ref, ids_ref, gate_ref, wg_hbm, wu_hbm, wd_hbm, out_ref,
    wg, wu, wd, table, slot_t, tok2, xs, xg, slot_out, slot_in, xb, px, pr, x1, hidden,
    s1, r1, s2, r2, s3, r3, ret, back, mix, acc,
    w_sem, meta_send, meta_recv, tok_send, tok_recv, z_send, z_recv, slot_send, slot_recv,
    b1_send, b1_recv, b2_send, b2_recv, ring_send, ring_recv, tail_send, tail_recv, x_send, x_recv,
    g1_send, g1_recv, g2_send, g2_recv, r1_send, r1_recv, r2_send, r2_recv, r3_send, r3_recv,
    back_send, back_recv,
):
    sec, e, t = lax.axis_index("section"), lax.axis_index("expert"), lax.axis_index("tensor")
    z, xh = lax.div(e, 2), lax.rem(e, 2)
    rows, quarter = tok_ref.shape
    half = quarter // 2
    late = xg.shape[3]
    pair = 2 * CAP
    right, left, opposite = lax.rem(t + 1, ny), lax.rem(t + ny - 1, ny), lax.rem(t + 2, ny)
    after, before = lax.rem(sec + 1, nsec), lax.rem(sec + nsec - 1, nsec)

    def away(k):
        return lax.rem(lax.div(k + 1, 2) * (2 * lax.rem(k, 2) - 1) + nz, nz)

    def z_to(k):
        return lax.rem(z + away(k), nz)

    def z_from(k):
        return lax.rem(z - away(k) + nz, nz)

    order = order_of(nz)
    packed = sum(k << (3 * p) for p, k in enumerate(order))

    def chunk_at(p):
        return lax.rem(lax.shift_right_logical(packed, 3 * p), 8)

    loads = [
        pltpu.make_async_copy(wg_hbm, wg, w_sem.at[0]),
        pltpu.make_async_copy(wu_hbm, wu, w_sem.at[1]),
    ] + [
        pltpu.make_async_copy(wd_hbm.at[:, pl.ds(q * quarter, quarter)], wd.at[q], w_sem.at[2 + q])
        for q in range(ny)
    ]
    for load in loads:
        load.start()

    named = iota((NAMES, rows), 0)
    own = jnp.zeros((NAMES, rows), F32)
    for k in range(ids_ref.shape[0]):
        own = own + jnp.where(ids_ref[k : k + 1, :] == named, gate_ref[k : k + 1, :], 0.0)
    table[xh] = own

    barrier = pltpu.get_barrier_semaphore()

    def greet(device):
        pl.semaphore_signal(barrier, inc=1, device_id=device, device_id_type=pl.DeviceIdType.MESH)

    partner = (sec, z * 2 + 1 - xh, t)
    to_right, to_left = (sec, e, right), (sec, e, left)
    greet(to_right)
    greet(to_left)
    greet(partner)
    for k in range(1, nz):
        greet((sec, z_from(k) * 2 + xh, t))
    for other in range(2 * nz):
        greet((before, other, t))
    pl.semaphore_wait(barrier, (nz - 1) + 3 + 2 * nz)

    def push(src, dst, send, recv, device):
        return pltpu.make_async_remote_copy(
            src_ref=src, dst_ref=dst, send_sem=send, recv_sem=recv,
            device_id=device, device_id_type=pl.DeviceIdType.MESH,
        )

    def both_ways(a, b, send, recv, k):
        return (
            push(a[0], a[1], send.at[0, k], recv.at[0, k], to_right),
            push(b[0], b[1], send.at[1, k], recv.at[1, k], to_left),
        )

    def start(copies):
        for copy in copies:
            copy.start()

    def arrive(copies):
        for copy in copies:
            copy.wait_recv()

    def early_out():
        a = (tok_ref.at[:, pl.ds(late, quarter - late)], xb.at[0, t])
        return both_ways(a, a, b1_send, b1_recv, 0)

    def early_in():
        a, b = xb.at[0, left], xb.at[0, right]
        return both_ways((a, a), (b, b), b1_send, b1_recv, 0)

    def early_pass(from_left, from_right):
        a = xb.at[0, from_left, pl.ds(0, rows // 2)]
        b = xb.at[0, from_right, pl.ds(rows // 2, rows // 2)]
        return both_ways((a, a), (b, b), b2_send, b2_recv, 0)

    meta_x = push(table.at[xh], table.at[xh], meta_send.at[0], meta_recv.at[0], partner)
    meta_s = push(table.at[xh], table.at[2], meta_send.at[1], meta_recv.at[1], (after, e, t))
    late_part = tok_ref.at[:, pl.ds(0, late)]
    tok_x = push(late_part, tok2.at[xh], tok_send, tok_recv, partner)
    meta_x.start()
    tok_x.start()
    start(early_out())
    meta_s.start()
    tok2[xh] = tok_ref[:, :late]
    xb[0, t] = tok_ref[:, late:]

    earlier = (iota((rows, rows), 0) < iota((rows, rows), 1)).astype(BF16)

    def slots_by_expert(gates):
        names = (gates > 0).astype(F32)
        return jnp.where(names > 0, dot(names.astype(BF16), earlier), -1000.0)

    slot_t[xh] = slots_by_expert(own)
    push(table.at[1 - xh], table.at[1 - xh], meta_send.at[0], meta_recv.at[0], partner).wait_recv()
    slot_t[1 - xh] = slots_by_expert(table[1 - xh])
    arrive(early_in())
    start(early_pass(left, right))

    def to_z(k):
        return push(xs.at[k], xg.at[k, t], z_send.at[k], z_recv.at[k], (sec, z_to(k) * 2 + xh, t))

    def slots_to_z(k):
        return push(
            slot_out.at[k], slot_in.at[k], slot_send.at[k], slot_recv.at[k],
            (sec, z_to(k) * 2 + xh, t),
        )

    def picked(slots, shift, count):
        return (slots + shift == iota((count, rows), 0).astype(F32)).astype(BF16)

    def pick(k):
        expert = z_to(k) * 2 + xh
        chosen = [picked(slot_t[j, pl.ds(expert, 1), :], float(CAP * j), pair) for j in range(2)]
        return (dot(chosen[0], tok2[0]) + dot(chosen[1], tok2[1])).astype(BF16)

    def gather(k):
        a = xg.at[k, t]
        return both_ways((a, a), (a, a), g1_send, g1_recv, k)

    def gathered(k):
        a, b = xg.at[k, left], xg.at[k, right]
        return both_ways((a, a), (b, b), g1_send, g1_recv, k)

    def forward(k, from_left, from_right):
        a = xg.at[k, from_left, pl.ds(0, PAD)]
        b = xg.at[k, from_right, pl.ds(PAD, pair - PAD)]
        return both_ways((a, a), (b, b), g2_send, g2_recv, k)

    push(late_part, tok2.at[1 - xh], tok_send, tok_recv, partner).wait_recv()
    xg[0, t] = pick(0)
    start(gather(0))

    def ring_next(k):
        dz = 2 * lax.rem(k, 2) - 1
        device = (sec, lax.rem(z + dz + nz, nz) * 2 + xh, t)
        return push(xb.at[k], xb.at[k + 2], ring_send.at[k], ring_recv.at[k + 2], device)

    up_z, down_z = (sec, lax.rem(z + 1, nz) * 2 + xh, t), (sec, lax.rem(z + nz - 1, nz) * 2 + xh, t)

    def ring_first():
        return (
            push(xb.at[0], xb.at[1], ring_send.at[nz - 2], ring_recv.at[1], up_z),
            push(xb.at[0], xb.at[2], ring_send.at[nz - 1], ring_recv.at[2], down_z),
        )

    def ring_in(k):
        return push(xb.at[0], xb.at[k], ring_send.at[0], ring_recv.at[k], up_z)

    def ring_last(j):
        part = pl.ds(j * (ny // 2), ny // 2)
        return push(
            xb.at[nz - 3 + j, part], xb.at[nz - 1, part], tail_send.at[j], tail_recv.at[j],
            (up_z, down_z)[j],
        )

    def over_x(k):
        return push(px.at[k], pr.at[k], x_send.at[k], x_recv.at[k], partner)

    def pick_for_partner(k):
        chosen = picked(slot_in[k, pl.ds(1 - xh, 1), :], ((PAD - CAP) * xh).astype(F32), PAD)
        for q in range(ny):
            px[k, q] = dot(chosen, xb[k, q]).astype(BF16)
        over_x(k).start()

    slot_in[0, 0:1, :] = slot_t[xh, pl.ds(z * 2, 1), :]
    slot_in[0, 1:2, :] = slot_t[xh, pl.ds(z * 2 + 1, 1), :]
    def send_stage(k):
        xs[k] = pick(k)
        to_z(k).start()

    for p in (1, 2):
        if p < nz:
            send_stage(jnp.int32(order[p]))

    arrive(early_pass(opposite, opposite))
    start(ring_first())

    def send_slots(k, carry):
        for j in range(2):
            slot_out[k, j : j + 1, :] = slot_t[xh, pl.ds(z_to(k) * 2 + j, 1), :]
        slots_to_z(k).start()
        return carry

    lax.fori_loop(1, nz, send_slots, 0)
    pick_for_partner(0)

    for load in loads:
        load.wait()

    def build_all_mix():
        push(table.at[2], table.at[2], meta_send.at[1], meta_recv.at[1], (after, e, t)).wait_recv()
        filler = jnp.zeros((128 - NAMES, rows), F32)
        gates = jnp.transpose(jnp.concatenate([table[2], filler], axis=0))
        slots = jnp.transpose(jnp.concatenate([slots_by_expert(table[2]), filler], axis=0))
        lanes = iota((rows, 128), 1)
        place = iota((rows, 2 * PAD), 1).astype(F32)

        def build_mix(k, carry):
            total = jnp.zeros((rows, 2 * PAD), F32)
            for j in range(2):
                here = lanes == z_to(k) * 2 + j
                gate = jnp.sum(jnp.where(here, gates, 0.0), axis=1, keepdims=True)
                slot = jnp.sum(jnp.where(here, slots, 0.0), axis=1, keepdims=True)
                at = slot + ((PAD - CAP) * xh).astype(F32) + float(PAD * j)
                total = total + jnp.where(place == at, gate, 0.0)
            high = total.astype(BF16)
            mix[k, 0] = high
            mix[k, 1] = (total - high.astype(F32)).astype(BF16)
            return carry

        lax.fori_loop(0, nz, build_mix, 0)
        acc[...] = jnp.zeros_like(acc)

    def relay(k):
        return both_ways((s1.at[0, k], r1.at[0, k]), (s1.at[1, k], r1.at[1, k]), r1_send, r1_recv, k)

    def direct(k):
        return both_ways((s2.at[0, k], r2.at[0, k]), (s2.at[1, k], r2.at[1, k]), r2_send, r2_recv, k)

    def joined(k):
        return both_ways((s3.at[0, k], r3.at[0, k]), (s3.at[1, k], r3.at[1, k]), r3_send, r3_recv, k)

    def give_back(k):
        return tuple(
            push(
                ret.at[k, pl.ds((pair - PAD) * j, PAD)], back.at[k, pl.ds(PAD * xh, PAD)],
                back_send.at[j, k], back_recv.at[xh, k], (after, z_from(k) * 2 + j, t),
            )
            for j in range(2)
        )

    def given_back(k):
        return tuple(
            push(
                ret.at[k, pl.ds((pair - PAD) * j, PAD)], back.at[k, pl.ds(PAD * j, PAD)],
                back_send.at[j, k], back_recv.at[j, k], to_right,
            )
            for j in range(2)
        )

    def ring_stage(k):
        @pl.when(k < nz - 1)
        def _():
            ring_in(k).wait_recv()

        @pl.when(k < nz - 3)
        def _():
            ring_next(k).start()

        for j in range(2):
            @pl.when(k == nz - 3 + j)
            def _(j=j):
                ring_last(j).start()

        @pl.when(k == nz - 1)
        def _():
            ring_last(0).wait_recv()
            ring_last(1).wait_recv()

    def partner_stage(k):
        slots_to_z(k).wait_recv()
        pick_for_partner(k)

    def gather_stage(k):
        push(xs.at[k], xg.at[k, t], z_send.at[k], z_recv.at[k], to_right).wait_recv()
        start(gather(k))

    def forward_stage(k):
        arrive(gathered(k))
        start(forward(k, left, right))

    def up_stage(k):
        arrive(forward(k, opposite, opposite))
        over_x(k).wait_recv()
        chosen = picked(slot_in[k, pl.ds(xh, 1), :], (CAP * xh).astype(F32), pair)
        theirs = pl.ds(pl.multiple_of((pair - PAD) * (1 - xh), 16), PAD)
        for q in range(ny):
            x1[q] = dot(chosen, xb[k, q]).astype(BF16)
            x1[q, theirs] = x1[q, theirs] + pr[k, q]
        gate_act = up_act = None
        for q in range(ny):
            for x, first, count in (
                (xg[k, q], q * quarter, late), (x1[q], q * quarter + late, quarter - late)
            ):
                g = dot(x, wg[first : first + count, :])
                u = dot(x, wu[first : first + count, :])
                gate_act = g if gate_act is None else gate_act + g
                up_act = u if up_act is None else up_act + u
        hidden[k] = (gate_act / (1.0 + jnp.exp(-gate_act)) * up_act).astype(BF16)
        part = dot(hidden[k], wd[opposite]).astype(BF16)
        s1[0, k] = part[:, :half]
        s1[1, k] = part[:, half:]
        start(relay(k))
        s2[0, k] = dot(hidden[k], wd[right, :, half:]).astype(BF16)
        s2[1, k] = dot(hidden[k], wd[left, :, :half]).astype(BF16)
        start(direct(k))

    def down_stage(k):
        arrive(relay(k))
        h = hidden[k]
        s3[0, k] = (dot(h, wd[right, :, :half]) + r1[0, k].astype(F32)).astype(BF16)
        s3[1, k] = (dot(h, wd[left, :, half:]) + r1[1, k].astype(F32)).astype(BF16)
        start(joined(k))

    def sum_stage(k):
        arrive(direct(k))
        arrive(joined(k))
        part = dot(hidden[k], wd[t])
        ret[k, :, :half] = (part[:, :half] + r3[0, k].astype(F32) + r2[1, k].astype(F32)).astype(BF16)
        ret[k, :, half:] = (part[:, half:] + r2[0, k].astype(F32) + r3[1, k].astype(F32)).astype(BF16)
        start(give_back(k))

    def mix_stage(k):
        arrive(given_back(k))
        y = back[k]
        acc[...] += dot(mix[k, 0], y) + dot(mix[k, 1], y)

    def leave(copies):
        for copy in copies:
            copy.wait_send()

    def drain_stage(k):
        @pl.when(k > 0)
        def _():
            leave((to_z(k), slots_to_z(k)))

        @pl.when((k > 0) & (k < nz - 3))
        def _():
            ring_next(k).wait_send()

        for copies in (
            gather(k), forward(k, left, right), relay(k), direct(k), joined(k), give_back(k),
        ):
            leave(copies)
        over_x(k).wait_send()

    def staged(i, lag, stage, first):
        p = i - lag

        @pl.when((p >= first) & (p < nz))
        def _():
            stage(chunk_at(p))

    def step(i, carry):
        staged(i, 2, sum_stage, 0)
        staged(i, 1, down_stage, 0)
        staged(i, 0, up_stage, 0)
        staged(i, -1, forward_stage, 0)
        staged(i, -4, send_stage, 3)

        @pl.when(i == 1)
        def _():
            build_all_mix()

        @pl.when(i < nz // 2 - 1)
        def _():
            ring_stage(2 * i + 3)

        @pl.when(i < nz // 2 - 2)
        def _():
            ring_stage(2 * i + 4)

        staged(i, -2, partner_stage, 1)
        staged(i, -2, gather_stage, 1)
        staged(i, 6, mix_stage, 0)
        staged(i, 6, drain_stage, 0)
        return carry

    lax.fori_loop(-1, nz + 6, step, 0)
    out_ref[...] = acc[...].astype(out_ref.dtype)

    leave((meta_x, meta_s, tok_x))
    leave(early_out())
    leave(early_pass(left, right))
    leave(ring_first())
    leave((ring_last(0), ring_last(1)))


def on_device(nsec, nz, ny, tokens, expert_ids, gate_values, w_gate, w_up, w_down):
    rows, quarter = tokens.shape[1:]
    width, units = w_gate.shape[2:]
    pair, half = 2 * CAP, quarter // 2
    late = quarter // 2
    early = quarter - late
    dma = pltpu.SemaphoreType.DMA
    vmem = lambda *shape, dtype=BF16: pltpu.VMEM(shape, dtype)
    sides = lambda n: [dma((2, n)), dma((2, n))]
    each = lambda n: [dma((n,)), dma((n,))]
    combined = pl.pallas_call(
        functools.partial(moe_kernel, nsec, nz, ny),
        out_shape=jax.ShapeDtypeStruct((rows, quarter), BF16),
        in_specs=[pl.BlockSpec(memory_space=pltpu.VMEM)] * 3 + [pl.BlockSpec(memory_space=pl.ANY)] * 3,
        out_specs=pl.BlockSpec(memory_space=pltpu.VMEM),
        scratch_shapes=[
            vmem(width, units), vmem(width, units), vmem(ny, units, quarter),
            vmem(3, NAMES, rows, dtype=F32),
            vmem(2, NAMES, rows, dtype=F32),
            vmem(2, rows, late),
            vmem(nz, pair, late),
            vmem(nz, ny, pair, late),
            vmem(nz, 8, rows, dtype=F32), vmem(nz, 8, rows, dtype=F32),
            vmem(nz, ny, rows, early),
            vmem(nz, ny, PAD, early), vmem(nz, ny, PAD, early),
            vmem(ny, pair, early),
            vmem(nz, pair, units),
            vmem(2, nz, pair, half), vmem(2, nz, pair, half),
            vmem(2, nz, pair, half), vmem(2, nz, pair, half),
            vmem(2, nz, pair, half), vmem(2, nz, pair, half),
            vmem(nz, pair, quarter),
            vmem(nz, 2 * PAD, quarter),
            vmem(nz, 2, rows, 2 * PAD),
            vmem(rows, quarter, dtype=F32),
            dma((2 + ny,)), *each(2), dma, dma, *each(nz), *each(nz),
            *sides(1), *sides(1), *each(nz), *each(2), *each(nz),
            *sides(nz), *sides(nz), *sides(nz), *sides(nz), *sides(nz),
            *sides(nz),
        ],
        compiler_params=pltpu.CompilerParams(
            collective_id=0, has_side_effects=True, vmem_limit_bytes=60 * 1024 * 1024
        ),
        cost_estimate=pl.CostEstimate(
            flops=6 * nz * pair * width * units, bytes_accessed=6 * width * units, transcendentals=0
        ),
    )(tokens[0], expert_ids[0].T, gate_values[0].T, w_gate[0, 0], w_up[0, 0], w_down[0, 0])
    return combined[None]


def solution(mesh):
    nsec, nexp, ny = mesh.shape["section"], mesh.shape["expert"], mesh.shape["tensor"]
    in_specs = (
        P("section", "expert", "tensor"),
        P("section", "expert", None),
        P("section", "expert", None),
        P("section", "expert", None, "tensor"),
        P("section", "expert", None, "tensor"),
        P("section", "expert", "tensor", None),
    )
    return jax.shard_map(
        functools.partial(on_device, nsec, nexp // 2, ny),
        mesh=mesh, in_specs=in_specs, out_specs=P("section", "expert", "tensor"), check_vma=False,
    )
```

```python
import functools

import jax
import jax.numpy as jnp
from jax import lax
from jax.experimental import pallas as pl
from jax.experimental.pallas import tpu as pltpu
from jax.sharding import PartitionSpec as P

CAP = 72
PAD = 80
NAMES = 16
BF16 = jnp.bfloat16
F32 = jnp.float32


def iota(shape, dim):
    return lax.broadcasted_iota(jnp.int32, shape, dim)


def dot(a, b):
    return jnp.dot(a, b, preferred_element_type=F32)


def order_of(nz):
    return {2: (0, 1), 4: (0, 1, 3, 2), 8: (0, 1, 4, 5, 6, 7, 3, 2)}[nz]


def moe_kernel(
    nsec, nz, ny,
    tok_ref, ids_ref, gate_ref, wg_hbm, wu_hbm, wd_hbm, out_ref,
    wgu, wd, table, slot_t, tok2, xs, xg, slot_out, slot_in, xb, px, pr, hidden,
    s1, r1, s2, r2, s3, r3, ret, back, mix, acc,
    w_sem, meta_send, meta_recv, tok_send, tok_recv, z_send, z_recv, slot_send, slot_recv,
    b1_send, b1_recv, b2_send, b2_recv, ring_send, ring_recv, tail_send, tail_recv, x_send, x_recv,
    g1_send, g1_recv, g2_send, g2_recv, r1_send, r1_recv, r2_send, r2_recv, r3_send, r3_recv,
    back_send, back_recv,
):
    sec, e, t = lax.axis_index("section"), lax.axis_index("expert"), lax.axis_index("tensor")
    z, xh = lax.div(e, 2), lax.rem(e, 2)
    rows, quarter = tok_ref.shape
    half, units = quarter // 2, hidden.shape[2]
    late = xs.shape[2]
    pair = 2 * CAP
    right, left, opposite = lax.rem(t + 1, ny), lax.rem(t + ny - 1, ny), lax.rem(t + 2, ny)
    after, before = lax.rem(sec + 1, nsec), lax.rem(sec + nsec - 1, nsec)

    def away(k):
        return lax.rem(lax.div(k + 1, 2) * (2 * lax.rem(k, 2) - 1) + nz, nz)

    def z_to(k):
        return lax.rem(z + away(k), nz)

    def z_from(k):
        return lax.rem(z - away(k) + nz, nz)

    order = order_of(nz)
    packed = sum(k << (3 * p) for p, k in enumerate(order))

    def chunk_at(p):
        return lax.rem(lax.shift_right_logical(packed, 3 * p), 8)

    loads = [
        pltpu.make_async_copy(wg_hbm, wgu.at[:, pl.ds(0, units)], w_sem.at[0]),
        pltpu.make_async_copy(wu_hbm, wgu.at[:, pl.ds(units, units)], w_sem.at[1]),
    ] + [
        pltpu.make_async_copy(wd_hbm.at[:, pl.ds(q * quarter, quarter)], wd.at[q], w_sem.at[2 + q])
        for q in range(ny)
    ]
    for load in loads:
        load.start()

    named = iota((NAMES, rows), 0)
    own = jnp.zeros((NAMES, rows), F32)
    for k in range(ids_ref.shape[0]):
        own = own + jnp.where(ids_ref[k : k + 1, :] == named, gate_ref[k : k + 1, :], 0.0)
    table[xh] = own

    barrier = pltpu.get_barrier_semaphore()

    def greet(device):
        pl.semaphore_signal(barrier, inc=1, device_id=device, device_id_type=pl.DeviceIdType.MESH)

    partner = (sec, z * 2 + 1 - xh, t)
    to_right, to_left = (sec, e, right), (sec, e, left)
    greet(to_right)
    greet(to_left)
    greet(partner)
    for k in range(1, nz):
        greet((sec, z_from(k) * 2 + xh, t))
    for other in range(2 * nz):
        greet((before, other, t))
    pl.semaphore_wait(barrier, (nz - 1) + 3 + 2 * nz)

    def push(src, dst, send, recv, device):
        return pltpu.make_async_remote_copy(
            src_ref=src, dst_ref=dst, send_sem=send, recv_sem=recv,
            device_id=device, device_id_type=pl.DeviceIdType.MESH,
        )

    def both_ways(a, b, send, recv, k):
        return (
            push(a[0], a[1], send.at[0, k], recv.at[0, k], to_right),
            push(b[0], b[1], send.at[1, k], recv.at[1, k], to_left),
        )

    def start(copies):
        for copy in copies:
            copy.start()

    def arrive(copies):
        for copy in copies:
            copy.wait_recv()

    def early_out():
        a = (tok_ref.at[:, pl.ds(late, quarter - late)], xb.at[0, t])
        return both_ways(a, a, b1_send, b1_recv, 0)

    def early_in():
        a, b = xb.at[0, left], xb.at[0, right]
        return both_ways((a, a), (b, b), b1_send, b1_recv, 0)

    def early_pass(from_left, from_right):
        a = xb.at[0, from_left, pl.ds(0, rows // 2)]
        b = xb.at[0, from_right, pl.ds(rows // 2, rows // 2)]
        return both_ways((a, a), (b, b), b2_send, b2_recv, 0)

    meta_x = push(table.at[xh], table.at[xh], meta_send.at[0], meta_recv.at[0], partner)
    meta_s = push(table.at[xh], table.at[2], meta_send.at[1], meta_recv.at[1], (after, e, t))
    late_part = tok_ref.at[:, pl.ds(0, late)]
    tok_x = push(late_part, tok2.at[xh], tok_send, tok_recv, partner)
    meta_x.start()
    tok_x.start()
    start(early_out())
    meta_s.start()
    tok2[xh] = tok_ref[:, :late]
    xb[0, t] = tok_ref[:, late:]

    earlier = (iota((rows, rows), 0) < iota((rows, rows), 1)).astype(BF16)

    def slots_by_expert(gates):
        names = (gates > 0).astype(F32)
        return jnp.where(names > 0, dot(names.astype(BF16), earlier), -1000.0)

    slot_t[xh] = slots_by_expert(own)
    push(table.at[1 - xh], table.at[1 - xh], meta_send.at[0], meta_recv.at[0], partner).wait_recv()
    slot_t[1 - xh] = slots_by_expert(table[1 - xh])
    arrive(early_in())
    start(early_pass(left, right))

    def late_of(k, q):
        return xg.at[k, q, :, pl.ds(0, late)]

    def to_z(k):
        return push(xs.at[k], late_of(k, t), z_send.at[k], z_recv.at[k], (sec, z_to(k) * 2 + xh, t))

    def slots_to_z(k):
        return push(
            slot_out.at[k], slot_in.at[k], slot_send.at[k], slot_recv.at[k],
            (sec, z_to(k) * 2 + xh, t),
        )

    def picked(slots, shift, count):
        return (slots + shift == iota((count, rows), 0).astype(F32)).astype(BF16)

    def pick(k):
        expert = z_to(k) * 2 + xh
        chosen = [picked(slot_t[j, pl.ds(expert, 1), :], float(CAP * j), pair) for j in range(2)]
        return (dot(chosen[0], tok2[0]) + dot(chosen[1], tok2[1])).astype(BF16)

    def gather(k):
        a = late_of(k, t)
        return both_ways((a, a), (a, a), g1_send, g1_recv, k)

    def gathered(k):
        a, b = late_of(k, left), late_of(k, right)
        return both_ways((a, a), (b, b), g1_send, g1_recv, k)

    def forward(k, from_left, from_right):
        a = xg.at[k, from_left, pl.ds(0, PAD), pl.ds(0, late)]
        b = xg.at[k, from_right, pl.ds(PAD, pair - PAD), pl.ds(0, late)]
        return both_ways((a, a), (b, b), g2_send, g2_recv, k)

    push(late_part, tok2.at[1 - xh], tok_send, tok_recv, partner).wait_recv()
    xg[0, t, :, :late] = pick(0)
    start(gather(0))

    def ring_next(k):
        dz = 2 * lax.rem(k, 2) - 1
        device = (sec, lax.rem(z + dz + nz, nz) * 2 + xh, t)
        return push(xb.at[k], xb.at[k + 2], ring_send.at[k], ring_recv.at[k + 2], device)

    up_z, down_z = (sec, lax.rem(z + 1, nz) * 2 + xh, t), (sec, lax.rem(z + nz - 1, nz) * 2 + xh, t)

    def ring_first():
        return (
            push(xb.at[0], xb.at[1], ring_send.at[nz - 2], ring_recv.at[1], up_z),
            push(xb.at[0], xb.at[2], ring_send.at[nz - 1], ring_recv.at[2], down_z),
        )

    def ring_in(k):
        return push(xb.at[0], xb.at[k], ring_send.at[0], ring_recv.at[k], up_z)

    def ring_last(j):
        part = pl.ds(j * (ny // 2), ny // 2)
        return push(
            xb.at[nz - 3 + j, part], xb.at[nz - 1, part], tail_send.at[j], tail_recv.at[j],
            (up_z, down_z)[j],
        )

    def over_x(k):
        return push(px.at[k], pr.at[k], x_send.at[k], x_recv.at[k], partner)

    def pick_for_partner(k):
        chosen = picked(slot_in[k, pl.ds(1 - xh, 1), :], ((PAD - CAP) * xh).astype(F32), PAD)
        for q in range(ny):
            px[k, q] = dot(chosen, xb[k, q]).astype(BF16)
        over_x(k).start()

    slot_in[0, 0:1, :] = slot_t[xh, pl.ds(z * 2, 1), :]
    slot_in[0, 1:2, :] = slot_t[xh, pl.ds(z * 2 + 1, 1), :]
    def send_stage(k):
        xs[k] = pick(k)
        to_z(k).start()

    for p in (1, 2):
        if p < nz:
            send_stage(jnp.int32(order[p]))

    arrive(early_pass(opposite, opposite))
    start(ring_first())

    def send_slots(k, carry):
        for j in range(2):
            slot_out[k, j : j + 1, :] = slot_t[xh, pl.ds(z_to(k) * 2 + j, 1), :]
        slots_to_z(k).start()
        return carry

    lax.fori_loop(1, nz, send_slots, 0)
    pick_for_partner(0)

    for load in loads:
        load.wait()

    def build_all_mix():
        push(table.at[2], table.at[2], meta_send.at[1], meta_recv.at[1], (after, e, t)).wait_recv()
        filler = jnp.zeros((128 - NAMES, rows), F32)
        gates = jnp.transpose(jnp.concatenate([table[2], filler], axis=0))
        slots = jnp.transpose(jnp.concatenate([slots_by_expert(table[2]), filler], axis=0))
        lanes = iota((rows, 128), 1)
        place = iota((rows, 2 * PAD), 1).astype(F32)

        def build_mix(k, carry):
            total = jnp.zeros((rows, 2 * PAD), F32)
            for j in range(2):
                here = lanes == z_to(k) * 2 + j
                gate = jnp.sum(jnp.where(here, gates, 0.0), axis=1, keepdims=True)
                slot = jnp.sum(jnp.where(here, slots, 0.0), axis=1, keepdims=True)
                at = slot + ((PAD - CAP) * xh).astype(F32) + float(PAD * j)
                total = total + jnp.where(place == at, gate, 0.0)
            high = total.astype(BF16)
            mix[k, 0] = high
            mix[k, 1] = (total - high.astype(F32)).astype(BF16)
            return carry

        lax.fori_loop(0, nz, build_mix, 0)
        acc[...] = jnp.zeros_like(acc)

    def relay(k):
        return both_ways((s1.at[0, k], r1.at[0, k]), (s1.at[1, k], r1.at[1, k]), r1_send, r1_recv, k)

    def direct(k):
        return both_ways((s2.at[0, k], r2.at[0, k]), (s2.at[1, k], r2.at[1, k]), r2_send, r2_recv, k)

    def joined(k):
        return both_ways((s3.at[0, k], r3.at[0, k]), (s3.at[1, k], r3.at[1, k]), r3_send, r3_recv, k)

    def give_back(k):
        return tuple(
            push(
                ret.at[k, pl.ds((pair - PAD) * j, PAD)], back.at[k, pl.ds(PAD * xh, PAD)],
                back_send.at[j, k], back_recv.at[xh, k], (after, z_from(k) * 2 + j, t),
            )
            for j in range(2)
        )

    def given_back(k):
        return tuple(
            push(
                ret.at[k, pl.ds((pair - PAD) * j, PAD)], back.at[k, pl.ds(PAD * j, PAD)],
                back_send.at[j, k], back_recv.at[j, k], to_right,
            )
            for j in range(2)
        )

    def ring_stage(k):
        @pl.when(k < nz - 1)
        def _():
            ring_in(k).wait_recv()

        @pl.when(k < nz - 3)
        def _():
            ring_next(k).start()

        for j in range(2):
            @pl.when(k == nz - 3 + j)
            def _(j=j):
                ring_last(j).start()

        @pl.when(k == nz - 1)
        def _():
            ring_last(0).wait_recv()
            ring_last(1).wait_recv()

    def partner_stage(k):
        slots_to_z(k).wait_recv()
        pick_for_partner(k)

    def gather_stage(k):
        push(xs.at[k], late_of(k, t), z_send.at[k], z_recv.at[k], to_right).wait_recv()
        start(gather(k))

    def forward_stage(k):
        arrive(gathered(k))
        start(forward(k, left, right))

    def up_stage(k):
        arrive(forward(k, opposite, opposite))
        over_x(k).wait_recv()
        chosen = picked(slot_in[k, pl.ds(xh, 1), :], (CAP * xh).astype(F32), pair)
        theirs = pl.ds(pl.multiple_of((pair - PAD) * (1 - xh), 16), PAD)
        for q in range(ny):
            xg[k, q, :, late:] = dot(chosen, xb[k, q]).astype(BF16)
            xg[k, q, theirs, late:] = xg[k, q, theirs, late:] + pr[k, q]
        acts = dot(xg[k, 0], wgu[:quarter, :])
        for q in range(1, ny):
            acts = acts + dot(xg[k, q], wgu[q * quarter : (q + 1) * quarter, :])
        gate_act, up_act = acts[:, :units], acts[:, units:]
        hidden[k] = (gate_act / (1.0 + jnp.exp(-gate_act)) * up_act).astype(BF16)
        part = dot(hidden[k], wd[opposite]).astype(BF16)
        s1[0, k] = part[:, :half]
        s1[1, k] = part[:, half:]
        start(relay(k))
        s2[0, k] = dot(hidden[k], wd[right, :, half:]).astype(BF16)
        s2[1, k] = dot(hidden[k], wd[left, :, :half]).astype(BF16)
        start(direct(k))

    def down_stage(k):
        arrive(relay(k))
        h = hidden[k]
        s3[0, k] = (dot(h, wd[right, :, :half]) + r1[0, k].astype(F32)).astype(BF16)
        s3[1, k] = (dot(h, wd[left, :, half:]) + r1[1, k].astype(F32)).astype(BF16)
        start(joined(k))

    def sum_stage(k):
        arrive(direct(k))
        arrive(joined(k))
        part = dot(hidden[k], wd[t])
        ret[k, :, :half] = (part[:, :half] + r3[0, k].astype(F32) + r2[1, k].astype(F32)).astype(BF16)
        ret[k, :, half:] = (part[:, half:] + r2[0, k].astype(F32) + r3[1, k].astype(F32)).astype(BF16)
        start(give_back(k))

    def mix_stage(k):
        arrive(given_back(k))
        y = back[k]
        acc[...] += dot(mix[k, 0], y) + dot(mix[k, 1], y)

    def leave(copies):
        for copy in copies:
            copy.wait_send()

    def drain_stage(k):
        @pl.when(k > 0)
        def _():
            leave((to_z(k), slots_to_z(k)))

        @pl.when((k > 0) & (k < nz - 3))
        def _():
            ring_next(k).wait_send()

        for copies in (
            gather(k), forward(k, left, right), relay(k), direct(k), joined(k), give_back(k),
        ):
            leave(copies)
        over_x(k).wait_send()

    def staged(i, lag, stage, first):
        p = i - lag

        @pl.when((p >= first) & (p < nz))
        def _():
            stage(chunk_at(p))

    def step(i, carry):
        staged(i, 2, sum_stage, 0)
        staged(i, 1, down_stage, 0)
        staged(i, -1, forward_stage, 0)
        staged(i, 0, up_stage, 0)

        @pl.when((i >= 0) & (i < nz // 2))
        def _():
            ring_stage(2 * i + 1)

        @pl.when((i >= 0) & (i < nz // 2 - 1))
        def _():
            ring_stage(2 * i + 2)

        staged(i, -1, partner_stage, 1)
        staged(i, -2, gather_stage, 1)
        staged(i, -4, send_stage, 3)

        @pl.when(i == 1)
        def _():
            build_all_mix()

        staged(i, 4, mix_stage, 0)
        staged(i, 5, drain_stage, 0)
        return carry

    lax.fori_loop(-1, nz + 5, step, 0)
    out_ref[...] = acc[...].astype(out_ref.dtype)

    leave((meta_x, meta_s, tok_x))
    leave(early_out())
    leave(early_pass(left, right))
    leave(ring_first())
    leave((ring_last(0), ring_last(1)))


def on_device(nsec, nz, ny, tokens, expert_ids, gate_values, w_gate, w_up, w_down):
    rows, quarter = tokens.shape[1:]
    width, units = w_gate.shape[2:]
    pair, half = 2 * CAP, quarter // 2
    late = 5 * quarter // 8
    early = quarter - late
    dma = pltpu.SemaphoreType.DMA
    vmem = lambda *shape, dtype=BF16: pltpu.VMEM(shape, dtype)
    sides = lambda n: [dma((2, n)), dma((2, n))]
    each = lambda n: [dma((n,)), dma((n,))]
    combined = pl.pallas_call(
        functools.partial(moe_kernel, nsec, nz, ny),
        out_shape=jax.ShapeDtypeStruct((rows, quarter), BF16),
        in_specs=[pl.BlockSpec(memory_space=pltpu.VMEM)] * 3 + [pl.BlockSpec(memory_space=pl.ANY)] * 3,
        out_specs=pl.BlockSpec(memory_space=pltpu.VMEM),
        scratch_shapes=[
            vmem(width, 2 * units), vmem(ny, units, quarter),
            vmem(3, NAMES, rows, dtype=F32),
            vmem(2, NAMES, rows, dtype=F32),
            vmem(2, rows, late),
            vmem(nz, pair, late),
            vmem(nz, ny, pair, quarter),
            vmem(nz, 8, rows, dtype=F32), vmem(nz, 8, rows, dtype=F32),
            vmem(nz, ny, rows, early),
            vmem(nz, ny, PAD, early), vmem(nz, ny, PAD, early),
            vmem(nz, pair, units),
            vmem(2, nz, pair, half), vmem(2, nz, pair, half),
            vmem(2, nz, pair, half), vmem(2, nz, pair, half),
            vmem(2, nz, pair, half), vmem(2, nz, pair, half),
            vmem(nz, pair, quarter),
            vmem(nz, 2 * PAD, quarter),
            vmem(nz, 2, rows, 2 * PAD),
            vmem(rows, quarter, dtype=F32),
            dma((2 + ny,)), *each(2), dma, dma, *each(nz), *each(nz),
            *sides(1), *sides(1), *each(nz), *each(2), *each(nz),
            *sides(nz), *sides(nz), *sides(nz), *sides(nz), *sides(nz),
            *sides(nz),
        ],
        compiler_params=pltpu.CompilerParams(
            collective_id=0, has_side_effects=True, vmem_limit_bytes=60 * 1024 * 1024
        ),
        cost_estimate=pl.CostEstimate(
            flops=6 * nz * pair * width * units, bytes_accessed=6 * width * units, transcendentals=0
        ),
    )(tokens[0], expert_ids[0].T, gate_values[0].T, w_gate[0, 0], w_up[0, 0], w_down[0, 0])
    return combined[None]


def solution(mesh):
    nsec, nexp, ny = mesh.shape["section"], mesh.shape["expert"], mesh.shape["tensor"]
    in_specs = (
        P("section", "expert", "tensor"),
        P("section", "expert", None),
        P("section", "expert", None),
        P("section", "expert", None, "tensor"),
        P("section", "expert", None, "tensor"),
        P("section", "expert", "tensor", None),
    )
    return jax.shard_map(
        functools.partial(on_device, nsec, nexp // 2, ny),
        mesh=mesh, in_specs=in_specs, out_specs=P("section", "expert", "tensor"), check_vma=False,
    )
```

```python
import functools

import jax
import jax.numpy as jnp
from jax import lax
from jax.experimental import pallas as pl
from jax.experimental.pallas import tpu as pltpu
from jax.sharding import PartitionSpec as P

CAP = 72
MAIN = 64
TAIL = CAP - MAIN
NAMES = 16
BF16 = jnp.bfloat16
F32 = jnp.float32


def iota(shape, dim):
    return lax.broadcasted_iota(jnp.int32, shape, dim)


def dot(a, b):
    return jnp.dot(a, b, preferred_element_type=F32)


def order_of(nz):
    return {2: (0, 1), 4: (0, 1, 3, 2), 8: (0, 1, 4, 5, 6, 7, 3, 2)}[nz]


def moe_kernel(
    nsec, nz, ny,
    tok_ref, ids_ref, gate_ref, wg_hbm, wu_hbm, wd_hbm, out_ref,
    wgu, wd, table, slot_t, tok2, xs, xg, slot_out, slot_in, xb, px, pr, hidden,
    s1, r1, s2, r2, s3, r3, ret, back, mix, acc,
    w_sem, meta_send, meta_recv, tok_send, tok_recv, z_send, z_recv, slot_send, slot_recv,
    b1_send, b1_recv, b2_send, b2_recv, ring_send, ring_recv, tail_send, tail_recv, x_send, x_recv,
    g1_send, g1_recv, g2_send, g2_recv, r1_send, r1_recv, r2_send, r2_recv, r3_send, r3_recv,
    back_send, back_recv,
):
    sec, e, t = lax.axis_index("section"), lax.axis_index("expert"), lax.axis_index("tensor")
    z, xh = lax.div(e, 2), lax.rem(e, 2)
    rows, quarter = tok_ref.shape
    half, units = quarter // 2, hidden.shape[2]
    late = xs.shape[2]
    pair = 2 * CAP
    packed_rows = ny * MAIN
    right, left, opposite = lax.rem(t + 1, ny), lax.rem(t + ny - 1, ny), lax.rem(t + 2, ny)
    after, before = lax.rem(sec + 1, nsec), lax.rem(sec + nsec - 1, nsec)

    def away(k):
        return lax.rem(lax.div(k + 1, 2) * (2 * lax.rem(k, 2) - 1) + nz, nz)

    def z_to(k):
        return lax.rem(z + away(k), nz)

    def z_from(k):
        return lax.rem(z - away(k) + nz, nz)

    order = order_of(nz)
    packed = sum(k << (3 * p) for p, k in enumerate(order))

    def chunk_at(p):
        return lax.rem(lax.shift_right_logical(packed, 3 * p), 8)

    loads = [
        pltpu.make_async_copy(wg_hbm, wgu.at[:, pl.ds(0, units)], w_sem.at[0]),
        pltpu.make_async_copy(wu_hbm, wgu.at[:, pl.ds(units, units)], w_sem.at[1]),
    ] + [
        pltpu.make_async_copy(wd_hbm.at[:, pl.ds(q * quarter, quarter)], wd.at[q], w_sem.at[2 + q])
        for q in range(ny)
    ]
    for load in loads:
        load.start()

    named = iota((NAMES, rows), 0)
    own = jnp.zeros((NAMES, rows), F32)
    for k in range(ids_ref.shape[0]):
        own = own + jnp.where(ids_ref[k : k + 1, :] == named, gate_ref[k : k + 1, :], 0.0)
    table[xh] = own

    barrier = pltpu.get_barrier_semaphore()

    def greet(device):
        pl.semaphore_signal(barrier, inc=1, device_id=device, device_id_type=pl.DeviceIdType.MESH)

    partner = (sec, z * 2 + 1 - xh, t)
    to_right, to_left = (sec, e, right), (sec, e, left)
    greet(to_right)
    greet(to_left)
    greet(partner)
    for k in range(1, nz):
        greet((sec, z_from(k) * 2 + xh, t))
    for other in range(2 * nz):
        greet((before, other, t))
    pl.semaphore_wait(barrier, (nz - 1) + 3 + 2 * nz)

    def push(src, dst, send, recv, device):
        return pltpu.make_async_remote_copy(
            src_ref=src, dst_ref=dst, send_sem=send, recv_sem=recv,
            device_id=device, device_id_type=pl.DeviceIdType.MESH,
        )

    def both_ways(a, b, send, recv, k):
        return (
            push(a[0], a[1], send.at[0, k], recv.at[0, k], to_right),
            push(b[0], b[1], send.at[1, k], recv.at[1, k], to_left),
        )

    def start(copies):
        for copy in copies:
            copy.start()

    def arrive(copies):
        for copy in copies:
            copy.wait_recv()

    def early_out():
        a = (tok_ref.at[:, pl.ds(late, quarter - late)], xb.at[0, t])
        return both_ways(a, a, b1_send, b1_recv, 0)

    def early_in():
        a, b = xb.at[0, left], xb.at[0, right]
        return both_ways((a, a), (b, b), b1_send, b1_recv, 0)

    def early_pass(from_left, from_right):
        a = xb.at[0, from_left, pl.ds(0, rows // 2)]
        b = xb.at[0, from_right, pl.ds(rows // 2, rows // 2)]
        return both_ways((a, a), (b, b), b2_send, b2_recv, 0)

    meta_x = push(table.at[xh], table.at[xh], meta_send.at[0], meta_recv.at[0], partner)
    meta_s = push(table.at[xh], table.at[2], meta_send.at[1], meta_recv.at[1], (after, e, t))
    late_part = tok_ref.at[:, pl.ds(0, late)]
    tok_x = push(late_part, tok2.at[xh], tok_send, tok_recv, partner)
    meta_x.start()
    tok_x.start()
    start(early_out())
    meta_s.start()
    tok2[xh] = tok_ref[:, :late]
    xb[0, t] = tok_ref[:, late:]

    earlier = (iota((rows, rows), 0) < iota((rows, rows), 1)).astype(BF16)

    def slots_by_expert(gates):
        names = (gates > 0).astype(F32)
        return jnp.where(names > 0, dot(names.astype(BF16), earlier), -1000.0)

    slot_t[xh] = slots_by_expert(own)
    push(table.at[1 - xh], table.at[1 - xh], meta_send.at[0], meta_recv.at[0], partner).wait_recv()
    slot_t[1 - xh] = slots_by_expert(table[1 - xh])
    arrive(early_in())
    start(early_pass(left, right))

    def late_of(k, q):
        return xg.at[k, q, :, pl.ds(0, late)]

    def to_z(k):
        return push(xs.at[k], late_of(k, t), z_send.at[k], z_recv.at[k], (sec, z_to(k) * 2 + xh, t))

    def slots_to_z(k):
        return push(
            slot_out.at[k], slot_in.at[k], slot_send.at[k], slot_recv.at[k],
            (sec, z_to(k) * 2 + xh, t),
        )

    def picked(slots, shift, count):
        return (slots + shift == iota((count, rows), 0).astype(F32)).astype(BF16)

    def pick(k):
        expert = z_to(k) * 2 + xh
        chosen = [picked(slot_t[j, pl.ds(expert, 1), :], float(CAP * j), pair) for j in range(2)]
        return (dot(chosen[0], tok2[0]) + dot(chosen[1], tok2[1])).astype(BF16)

    def gather(k):
        a = late_of(k, t)
        return both_ways((a, a), (a, a), g1_send, g1_recv, k)

    def gathered(k):
        a, b = late_of(k, left), late_of(k, right)
        return both_ways((a, a), (b, b), g1_send, g1_recv, k)

    def forward(k, from_left, from_right):
        split = MAIN + 2 * TAIL
        a = xg.at[k, from_left, pl.ds(0, split), pl.ds(0, late)]
        b = xg.at[k, from_right, pl.ds(split, pair - split), pl.ds(0, late)]
        return both_ways((a, a), (b, b), g2_send, g2_recv, k)

    push(late_part, tok2.at[1 - xh], tok_send, tok_recv, partner).wait_recv()
    xg[0, t, :, :late] = pick(0)
    start(gather(0))

    def ring_next(k):
        dz = 2 * lax.rem(k, 2) - 1
        device = (sec, lax.rem(z + dz + nz, nz) * 2 + xh, t)
        return push(xb.at[k], xb.at[k + 2], ring_send.at[k], ring_recv.at[k + 2], device)

    up_z, down_z = (sec, lax.rem(z + 1, nz) * 2 + xh, t), (sec, lax.rem(z + nz - 1, nz) * 2 + xh, t)

    def ring_first():
        return (
            push(xb.at[0], xb.at[1], ring_send.at[nz - 2], ring_recv.at[1], up_z),
            push(xb.at[0], xb.at[2], ring_send.at[nz - 1], ring_recv.at[2], down_z),
        )

    def ring_in(k):
        return push(xb.at[0], xb.at[k], ring_send.at[0], ring_recv.at[k], up_z)

    def ring_last(j):
        part = pl.ds(j * (ny // 2), ny // 2)
        return push(
            xb.at[nz - 3 + j, part], xb.at[nz - 1, part], tail_send.at[j], tail_recv.at[j],
            (up_z, down_z)[j],
        )

    def over_x(k):
        return push(px.at[k], pr.at[k], x_send.at[k], x_recv.at[k], partner)

    def pick_for_partner(k):
        slots = slot_in[k, pl.ds(1 - xh, 1), :]
        main = picked(slots, (-TAIL * xh).astype(F32), MAIN)
        low = iota((2 * TAIL, rows), 0) < TAIL
        tail = picked(slots, (-MAIN * (1 - xh)).astype(F32), 2 * TAIL)
        tail_up = picked(slots, (TAIL - MAIN * (1 - xh)).astype(F32), 2 * TAIL)
        tails = (jnp.where(low, tail, 0).astype(BF16), jnp.where(low, 0, tail_up).astype(BF16))
        for q in range(ny):
            px[k, q * MAIN : (q + 1) * MAIN] = dot(main, xb[k, q]).astype(BF16)
        for j in range(ny // 2):
            both = dot(tails[0], xb[k, 2 * j]) + dot(tails[1], xb[k, 2 * j + 1])
            first = packed_rows + j * 2 * TAIL
            px[k, first : first + 2 * TAIL] = both.astype(BF16)
        over_x(k).start()

    slot_in[0, 0:1, :] = slot_t[xh, pl.ds(z * 2, 1), :]
    slot_in[0, 1:2, :] = slot_t[xh, pl.ds(z * 2 + 1, 1), :]
    def send_stage(k):
        xs[k] = pick(k)
        to_z(k).start()

    for p in (1, 2):
        if p < nz:
            send_stage(jnp.int32(order[p]))

    arrive(early_pass(opposite, opposite))
    start(ring_first())

    def send_slots(k, carry):
        for j in range(2):
            slot_out[k, j : j + 1, :] = slot_t[xh, pl.ds(z_to(k) * 2 + j, 1), :]
        slots_to_z(k).start()
        return carry

    lax.fori_loop(1, nz, send_slots, 0)
    pick_for_partner(0)

    for load in loads:
        load.wait()

    def build_all_mix():
        push(table.at[2], table.at[2], meta_send.at[1], meta_recv.at[1], (after, e, t)).wait_recv()
        filler = jnp.zeros((128 - NAMES, rows), F32)
        gates = jnp.transpose(jnp.concatenate([table[2], filler], axis=0))
        slots = jnp.transpose(jnp.concatenate([slots_by_expert(table[2]), filler], axis=0))
        lanes = iota((rows, 128), 1)
        place = iota((rows, 2 * pair), 1).astype(F32)

        def build_mix(k, carry):
            total = [jnp.zeros((rows, 2 * pair), F32) for _ in range(2)]
            for j in range(2):
                here = lanes == z_to(k) * 2 + j
                gate = jnp.sum(jnp.where(here, gates, 0.0), axis=1, keepdims=True)
                slot = jnp.sum(jnp.where(here, slots, 0.0), axis=1, keepdims=True)
                main = slot - (TAIL * xh).astype(F32)
                tail = slot - (MAIN * (1 - xh)).astype(F32)
                in_main = (main >= 0) & (main < MAIN)
                for side in range(2):
                    at = jnp.where(in_main, main + MAIN * side, tail + (2 * MAIN + TAIL * side))
                    total[side] = total[side] + jnp.where(place == at + pair * j, gate, 0.0)
            for side in range(2):
                high = total[side].astype(BF16)
                mix[k, side, 0] = high
                mix[k, side, 1] = (total[side] - high.astype(F32)).astype(BF16)
            return carry

        lax.fori_loop(0, nz, build_mix, 0)
        acc[...] = jnp.zeros_like(acc)

    def relay(k):
        return both_ways((s1.at[0, k], r1.at[0, k]), (s1.at[1, k], r1.at[1, k]), r1_send, r1_recv, k)

    def direct(k):
        return both_ways((s2.at[0, k], r2.at[0, k]), (s2.at[1, k], r2.at[1, k]), r2_send, r2_recv, k)

    def joined(k):
        return both_ways((s3.at[0, k], r3.at[0, k]), (s3.at[1, k], r3.at[1, k]), r3_send, r3_recv, k)

    def give_back(k):
        return tuple(
            push(
                ret.at[k, j], back.at[k, pl.ds(pair * xh, pair)],
                back_send.at[j, k], back_recv.at[xh, k], (after, z_from(k) * 2 + j, t),
            )
            for j in range(2)
        )

    def given_back(k):
        return tuple(
            push(
                ret.at[k, j], back.at[k, pl.ds(pair * j, pair)],
                back_send.at[j, k], back_recv.at[j, k], to_right,
            )
            for j in range(2)
        )

    def ring_stage(k):
        @pl.when(k < nz - 1)
        def _():
            ring_in(k).wait_recv()

        @pl.when(k < nz - 3)
        def _():
            ring_next(k).start()

        for j in range(2):
            @pl.when(k == nz - 3 + j)
            def _(j=j):
                ring_last(j).start()

        @pl.when(k == nz - 1)
        def _():
            ring_last(0).wait_recv()
            ring_last(1).wait_recv()

    def partner_stage(k):
        slots_to_z(k).wait_recv()
        pick_for_partner(k)

    def gather_stage(k):
        push(xs.at[k], late_of(k, t), z_send.at[k], z_recv.at[k], to_right).wait_recv()
        start(gather(k))

    def forward_stage(k):
        arrive(gathered(k))
        start(forward(k, left, right))

    def up_stage(k):
        arrive(forward(k, opposite, opposite))
        over_x(k).wait_recv()
        chosen = picked(slot_in[k, pl.ds(xh, 1), :], (CAP * xh).astype(F32), pair)
        theirs = pl.ds(pl.multiple_of((MAIN + 2 * TAIL) * (1 - xh), 16), MAIN)
        middle = slice(MAIN, MAIN + 2 * TAIL)
        r, c = iota((2 * TAIL, 2 * TAIL), 0), iota((2 * TAIL, 2 * TAIL), 1)
        mine = (r < TAIL) == (xh == 1)
        for q in range(ny):
            xg[k, q, :, late:] = dot(chosen, xb[k, q]).astype(BF16)
            xg[k, q, theirs, late:] = pr[k, q * MAIN : (q + 1) * MAIN]
            shift = (mine & (c == r + TAIL * (q % 2) - TAIL * (1 - xh))).astype(BF16)
            first = packed_rows + (q // 2) * 2 * TAIL
            moved = dot(shift, pr[k, first : first + 2 * TAIL]).astype(BF16)
            xg[k, q, middle, late:] = xg[k, q, middle, late:] + moved
        acts = dot(xg[k, 0], wgu[:quarter, :])
        for q in range(1, ny):
            acts = acts + dot(xg[k, q], wgu[q * quarter : (q + 1) * quarter, :])
        gate_act, up_act = acts[:, :units], acts[:, units:]
        hidden[k] = (gate_act / (1.0 + jnp.exp(-gate_act)) * up_act).astype(BF16)
        part = dot(hidden[k], wd[opposite]).astype(BF16)
        s1[0, k] = part[:, :half]
        s1[1, k] = part[:, half:]
        start(relay(k))
        s2[0, k] = dot(hidden[k], wd[right, :, half:]).astype(BF16)
        s2[1, k] = dot(hidden[k], wd[left, :, :half]).astype(BF16)
        start(direct(k))

    def down_stage(k):
        arrive(relay(k))
        h = hidden[k]
        s3[0, k] = (dot(h, wd[right, :, :half]) + r1[0, k].astype(F32)).astype(BF16)
        s3[1, k] = (dot(h, wd[left, :, half:]) + r1[1, k].astype(F32)).astype(BF16)
        start(joined(k))

    def sum_stage(k):
        arrive(direct(k))
        arrive(joined(k))
        part = dot(hidden[k], wd[t])
        lo = part[:, :half] + r3[0, k].astype(F32) + r2[1, k].astype(F32)
        hi = part[:, half:] + r2[0, k].astype(F32) + r3[1, k].astype(F32)
        for j in range(2):
            first, tail = (MAIN + 2 * TAIL) * j, MAIN + TAIL * j
            ret[k, j, :MAIN] = lo[first : first + MAIN].astype(BF16)
            ret[k, j, MAIN : 2 * MAIN] = hi[first : first + MAIN].astype(BF16)
            tails = jnp.concatenate([lo[tail : tail + TAIL], hi[tail : tail + TAIL]], axis=0)
            ret[k, j, 2 * MAIN :] = tails.astype(BF16)
        start(give_back(k))

    def mix_stage(k):
        arrive(given_back(k))
        y = back[k]
        acc[:, :half] += dot(mix[k, 0, 0], y) + dot(mix[k, 0, 1], y)
        acc[:, half:] += dot(mix[k, 1, 0], y) + dot(mix[k, 1, 1], y)

    def leave(copies):
        for copy in copies:
            copy.wait_send()

    def drain_stage(k):
        @pl.when(k > 0)
        def _():
            leave((to_z(k), slots_to_z(k)))

        @pl.when((k > 0) & (k < nz - 3))
        def _():
            ring_next(k).wait_send()

        for copies in (
            gather(k), forward(k, left, right), relay(k), direct(k), joined(k), give_back(k),
        ):
            leave(copies)
        over_x(k).wait_send()

    def staged(i, lag, stage, first):
        p = i - lag

        @pl.when((p >= first) & (p < nz))
        def _():
            stage(chunk_at(p))

    def step(i, carry):
        staged(i, 2, sum_stage, 0)
        staged(i, 1, down_stage, 0)
        staged(i, -1, forward_stage, 0)
        staged(i, 0, up_stage, 0)

        @pl.when((i >= 0) & (i < nz // 2))
        def _():
            ring_stage(2 * i + 1)

        @pl.when((i >= 0) & (i < nz // 2 - 1))
        def _():
            ring_stage(2 * i + 2)

        staged(i, -1, partner_stage, 1)
        staged(i, -2, gather_stage, 1)
        staged(i, -4, send_stage, 3)

        @pl.when(i == 1)
        def _():
            build_all_mix()

        staged(i, 4, mix_stage, 0)
        staged(i, 5, drain_stage, 0)
        return carry

    lax.fori_loop(-1, nz + 5, step, 0)
    out_ref[...] = acc[...].astype(out_ref.dtype)

    leave((meta_x, meta_s, tok_x))
    leave(early_out())
    leave(early_pass(left, right))
    leave(ring_first())
    leave((ring_last(0), ring_last(1)))


def on_device(nsec, nz, ny, tokens, expert_ids, gate_values, w_gate, w_up, w_down):
    rows, quarter = tokens.shape[1:]
    width, units = w_gate.shape[2:]
    pair, half = 2 * CAP, quarter // 2
    late = 5 * quarter // 8
    early = quarter - late
    dma = pltpu.SemaphoreType.DMA
    vmem = lambda *shape, dtype=BF16: pltpu.VMEM(shape, dtype)
    sides = lambda n: [dma((2, n)), dma((2, n))]
    each = lambda n: [dma((n,)), dma((n,))]
    combined = pl.pallas_call(
        functools.partial(moe_kernel, nsec, nz, ny),
        out_shape=jax.ShapeDtypeStruct((rows, quarter), BF16),
        in_specs=[pl.BlockSpec(memory_space=pltpu.VMEM)] * 3 + [pl.BlockSpec(memory_space=pl.ANY)] * 3,
        out_specs=pl.BlockSpec(memory_space=pltpu.VMEM),
        scratch_shapes=[
            vmem(width, 2 * units), vmem(ny, units, quarter),
            vmem(3, NAMES, rows, dtype=F32),
            vmem(2, NAMES, rows, dtype=F32),
            vmem(2, rows, late),
            vmem(nz, pair, late),
            vmem(nz, ny, pair, quarter),
            vmem(nz, 8, rows, dtype=F32), vmem(nz, 8, rows, dtype=F32),
            vmem(nz, ny, rows, early),
            vmem(nz, ny * CAP, early), vmem(nz, ny * CAP, early),
            vmem(nz, pair, units),
            vmem(2, nz, pair, half), vmem(2, nz, pair, half),
            vmem(2, nz, pair, half), vmem(2, nz, pair, half),
            vmem(2, nz, pair, half), vmem(2, nz, pair, half),
            vmem(nz, 2, pair, half),
            vmem(nz, 2 * pair, half),
            vmem(nz, 2, 2, rows, 2 * pair),
            vmem(rows, quarter, dtype=F32),
            dma((2 + ny,)), *each(2), dma, dma, *each(nz), *each(nz),
            *sides(1), *sides(1), *each(nz), *each(2), *each(nz),
            *sides(nz), *sides(nz), *sides(nz), *sides(nz), *sides(nz),
            *sides(nz),
        ],
        compiler_params=pltpu.CompilerParams(
            collective_id=0, has_side_effects=True, vmem_limit_bytes=60 * 1024 * 1024
        ),
        cost_estimate=pl.CostEstimate(
            flops=6 * nz * pair * width * units, bytes_accessed=6 * width * units, transcendentals=0
        ),
    )(tokens[0], expert_ids[0].T, gate_values[0].T, w_gate[0, 0], w_up[0, 0], w_down[0, 0])
    return combined[None]


def solution(mesh):
    nsec, nexp, ny = mesh.shape["section"], mesh.shape["expert"], mesh.shape["tensor"]
    in_specs = (
        P("section", "expert", "tensor"),
        P("section", "expert", None),
        P("section", "expert", None),
        P("section", "expert", None, "tensor"),
        P("section", "expert", None, "tensor"),
        P("section", "expert", "tensor", None),
    )
    return jax.shard_map(
        functools.partial(on_device, nsec, nexp // 2, ny),
        mesh=mesh, in_specs=in_specs, out_specs=P("section", "expert", "tensor"), check_vma=False,
    )
```

```python
import functools

import jax
import jax.numpy as jnp
from jax import lax
from jax.experimental import pallas as pl
from jax.experimental.pallas import tpu as pltpu
from jax.sharding import PartitionSpec as P

CAP = 72
MAIN = 64
TAIL = CAP - MAIN
NAMES = 16
BF16 = jnp.bfloat16
F32 = jnp.float32


def iota(shape, dim):
    return lax.broadcasted_iota(jnp.int32, shape, dim)


def dot(a, b):
    return jnp.dot(a, b, preferred_element_type=F32)


def order_of(nz):
    return {2: (0, 1), 4: (0, 1, 3, 2), 8: (0, 1, 4, 5, 6, 7, 3, 2)}[nz]


def moe_kernel(
    nsec, nz, ny,
    tok_ref, ids_ref, gate_ref, wg_hbm, wu_hbm, wd_hbm, out_ref,
    wgu, wd, table, slot_t, tok2, xs, xg, slot_out, slot_in, xb, px, pr, hidden,
    s1, r1, s2, r2, s3, r3, ret, back, turned, mix, acc,
    w_sem, meta_send, meta_recv, tok_send, tok_recv, z_send, z_recv, slot_send, slot_recv,
    b1_send, b1_recv, b2_send, b2_recv, ring_send, ring_recv, tail_send, tail_recv, x_send, x_recv,
    g1_send, g1_recv, g2_send, g2_recv, r1_send, r1_recv, r2_send, r2_recv, r3_send, r3_recv,
    back_send, back_recv,
):
    sec, e, t = lax.axis_index("section"), lax.axis_index("expert"), lax.axis_index("tensor")
    z, xh = lax.div(e, 2), lax.rem(e, 2)
    rows, quarter = tok_ref.shape
    half, units = quarter // 2, hidden.shape[2]
    late = xs.shape[2]
    pair = 2 * CAP
    packed_rows = ny * MAIN
    right, left, opposite = lax.rem(t + 1, ny), lax.rem(t + ny - 1, ny), lax.rem(t + 2, ny)
    after, before = lax.rem(sec + 1, nsec), lax.rem(sec + nsec - 1, nsec)

    def away(k):
        return lax.rem(lax.div(k + 1, 2) * (2 * lax.rem(k, 2) - 1) + nz, nz)

    def z_to(k):
        return lax.rem(z + away(k), nz)

    def z_from(k):
        return lax.rem(z - away(k) + nz, nz)

    order = order_of(nz)
    packed = sum(k << (3 * p) for p, k in enumerate(order))

    def chunk_at(p):
        return lax.rem(lax.shift_right_logical(packed, 3 * p), 8)

    loads = [
        pltpu.make_async_copy(wg_hbm, wgu.at[:, pl.ds(0, units)], w_sem.at[0]),
        pltpu.make_async_copy(wu_hbm, wgu.at[:, pl.ds(units, units)], w_sem.at[1]),
    ] + [
        pltpu.make_async_copy(wd_hbm.at[:, pl.ds(q * quarter, quarter)], wd.at[q], w_sem.at[2 + q])
        for q in range(ny)
    ]
    for load in loads:
        load.start()

    named = iota((NAMES, rows), 0)
    own = jnp.zeros((NAMES, rows), F32)
    for k in range(ids_ref.shape[0]):
        own = own + jnp.where(ids_ref[k : k + 1, :] == named, gate_ref[k : k + 1, :], 0.0)
    table[xh] = own

    barrier = pltpu.get_barrier_semaphore()

    def greet(device):
        pl.semaphore_signal(barrier, inc=1, device_id=device, device_id_type=pl.DeviceIdType.MESH)

    partner = (sec, z * 2 + 1 - xh, t)
    to_right, to_left = (sec, e, right), (sec, e, left)
    greet(to_right)
    greet(to_left)
    greet(partner)
    for k in range(1, nz):
        greet((sec, z_from(k) * 2 + xh, t))
    for other in range(2 * nz):
        greet((before, other, t))
    pl.semaphore_wait(barrier, (nz - 1) + 3 + 2 * nz)

    def push(src, dst, send, recv, device):
        return pltpu.make_async_remote_copy(
            src_ref=src, dst_ref=dst, send_sem=send, recv_sem=recv,
            device_id=device, device_id_type=pl.DeviceIdType.MESH,
        )

    def both_ways(a, b, send, recv, k):
        return (
            push(a[0], a[1], send.at[0, k], recv.at[0, k], to_right),
            push(b[0], b[1], send.at[1, k], recv.at[1, k], to_left),
        )

    def start(copies):
        for copy in copies:
            copy.start()

    def arrive(copies):
        for copy in copies:
            copy.wait_recv()

    def early_out():
        a = (tok_ref.at[:, pl.ds(late, quarter - late)], xb.at[0, t])
        return both_ways(a, a, b1_send, b1_recv, 0)

    def early_in():
        a, b = xb.at[0, left], xb.at[0, right]
        return both_ways((a, a), (b, b), b1_send, b1_recv, 0)

    def early_pass(from_left, from_right):
        a = xb.at[0, from_left, pl.ds(0, rows // 2)]
        b = xb.at[0, from_right, pl.ds(rows // 2, rows // 2)]
        return both_ways((a, a), (b, b), b2_send, b2_recv, 0)

    meta_x = push(table.at[xh], table.at[xh], meta_send.at[0], meta_recv.at[0], partner)
    meta_s = push(table.at[xh], table.at[2], meta_send.at[1], meta_recv.at[1], (after, e, t))
    late_part = tok_ref.at[:, pl.ds(0, late)]
    tok_x = push(late_part, tok2.at[xh], tok_send, tok_recv, partner)
    meta_x.start()
    tok_x.start()
    start(early_out())
    meta_s.start()
    tok2[xh] = tok_ref[:, :late]
    xb[0, t] = tok_ref[:, late:]

    earlier = (iota((rows, rows), 0) < iota((rows, rows), 1)).astype(BF16)

    def slots_by_expert(gates):
        names = (gates > 0).astype(F32)
        return jnp.where(names > 0, dot(names.astype(BF16), earlier), -1000.0)

    slot_t[xh] = slots_by_expert(own)
    push(table.at[1 - xh], table.at[1 - xh], meta_send.at[0], meta_recv.at[0], partner).wait_recv()
    slot_t[1 - xh] = slots_by_expert(table[1 - xh])
    arrive(early_in())
    start(early_pass(left, right))

    def late_of(k, q):
        return xg.at[k, q, :, pl.ds(0, late)]

    def to_z(k):
        return push(xs.at[k], late_of(k, t), z_send.at[k], z_recv.at[k], (sec, z_to(k) * 2 + xh, t))

    def slots_to_z(k):
        return push(
            slot_out.at[k], slot_in.at[k], slot_send.at[k], slot_recv.at[k],
            (sec, z_to(k) * 2 + xh, t),
        )

    def picked(slots, shift, count):
        return (slots + shift == iota((count, rows), 0).astype(F32)).astype(BF16)

    def pick(k):
        expert = z_to(k) * 2 + xh
        chosen = [picked(slot_t[j, pl.ds(expert, 1), :], float(CAP * j), pair) for j in range(2)]
        return (dot(chosen[0], tok2[0]) + dot(chosen[1], tok2[1])).astype(BF16)

    def gather(k):
        a = late_of(k, t)
        return both_ways((a, a), (a, a), g1_send, g1_recv, k)

    def gathered(k):
        a, b = late_of(k, left), late_of(k, right)
        return both_ways((a, a), (b, b), g1_send, g1_recv, k)

    def forward(k, from_left, from_right):
        split = MAIN + 2 * TAIL
        a = xg.at[k, from_left, pl.ds(0, split), pl.ds(0, late)]
        b = xg.at[k, from_right, pl.ds(split, pair - split), pl.ds(0, late)]
        return both_ways((a, a), (b, b), g2_send, g2_recv, k)

    push(late_part, tok2.at[1 - xh], tok_send, tok_recv, partner).wait_recv()
    xg[0, t, :, :late] = pick(0)
    start(gather(0))

    def ring_next(k):
        dz = 2 * lax.rem(k, 2) - 1
        device = (sec, lax.rem(z + dz + nz, nz) * 2 + xh, t)
        return push(xb.at[k], xb.at[k + 2], ring_send.at[k], ring_recv.at[k + 2], device)

    up_z, down_z = (sec, lax.rem(z + 1, nz) * 2 + xh, t), (sec, lax.rem(z + nz - 1, nz) * 2 + xh, t)

    def ring_first():
        return (
            push(xb.at[0], xb.at[1], ring_send.at[nz - 2], ring_recv.at[1], up_z),
            push(xb.at[0], xb.at[2], ring_send.at[nz - 1], ring_recv.at[2], down_z),
        )

    def ring_in(k):
        return push(xb.at[0], xb.at[k], ring_send.at[0], ring_recv.at[k], up_z)

    def ring_last(j):
        part = pl.ds(j * (ny // 2), ny // 2)
        return push(
            xb.at[nz - 3 + j, part], xb.at[nz - 1, part], tail_send.at[j], tail_recv.at[j],
            (up_z, down_z)[j],
        )

    def over_x(k):
        return push(px.at[k], pr.at[k], x_send.at[k], x_recv.at[k], partner)

    def pick_for_partner(k):
        slots = slot_in[k, pl.ds(1 - xh, 1), :]
        main = picked(slots, (-TAIL * xh).astype(F32), MAIN)
        low = iota((2 * TAIL, rows), 0) < TAIL
        tail = picked(slots, (-MAIN * (1 - xh)).astype(F32), 2 * TAIL)
        tail_up = picked(slots, (TAIL - MAIN * (1 - xh)).astype(F32), 2 * TAIL)
        tails = (jnp.where(low, tail, 0).astype(BF16), jnp.where(low, 0, tail_up).astype(BF16))
        for q in range(ny):
            px[k, q * MAIN : (q + 1) * MAIN] = dot(main, xb[k, q]).astype(BF16)
        for j in range(ny // 2):
            both = dot(tails[0], xb[k, 2 * j]) + dot(tails[1], xb[k, 2 * j + 1])
            first = packed_rows + j * 2 * TAIL
            px[k, first : first + 2 * TAIL] = both.astype(BF16)
        over_x(k).start()

    slot_in[0, 0:1, :] = slot_t[xh, pl.ds(z * 2, 1), :]
    slot_in[0, 1:2, :] = slot_t[xh, pl.ds(z * 2 + 1, 1), :]
    def send_stage(k):
        xs[k] = pick(k)
        to_z(k).start()

    for p in (1, 2):
        if p < nz:
            send_stage(jnp.int32(order[p]))

    arrive(early_pass(opposite, opposite))
    start(ring_first())

    def send_slots(k, carry):
        for j in range(2):
            slot_out[k, j : j + 1, :] = slot_t[xh, pl.ds(z_to(k) * 2 + j, 1), :]
        slots_to_z(k).start()
        return carry

    lax.fori_loop(1, nz, send_slots, 0)
    pick_for_partner(0)

    for load in loads:
        load.wait()

    def turn_tables():
        push(table.at[2], table.at[2], meta_send.at[1], meta_recv.at[1], (after, e, t)).wait_recv()
        filler = jnp.zeros((128 - NAMES, rows), F32)
        turned[0] = jnp.transpose(jnp.concatenate([table[2], filler], axis=0))
        turned[1] = jnp.transpose(jnp.concatenate([slots_by_expert(table[2]), filler], axis=0))
        acc[...] = jnp.zeros_like(acc)

    def weight_stage(k):
        lanes = iota((rows, 128), 1)
        place = iota((rows, 2 * pair), 1).astype(F32)
        total = [jnp.zeros((rows, 2 * pair), F32) for _ in range(2)]
        for j in range(2):
            here = lanes == z_to(k) * 2 + j
            gate = jnp.sum(jnp.where(here, turned[0], 0.0), axis=1, keepdims=True)
            slot = jnp.sum(jnp.where(here, turned[1], 0.0), axis=1, keepdims=True)
            main = slot - (TAIL * xh).astype(F32)
            tail = slot - (MAIN * (1 - xh)).astype(F32)
            in_main = (main >= 0) & (main < MAIN)
            for side in range(2):
                at = jnp.where(in_main, main + MAIN * side, tail + (2 * MAIN + TAIL * side))
                total[side] = total[side] + jnp.where(place == at + pair * j, gate, 0.0)
        for side in range(2):
            high = total[side].astype(BF16)
            mix[k, side, 0] = high
            mix[k, side, 1] = (total[side] - high.astype(F32)).astype(BF16)

    def relay(k):
        return both_ways((s1.at[0, k], r1.at[0, k]), (s1.at[1, k], r1.at[1, k]), r1_send, r1_recv, k)

    def direct(k):
        return both_ways((s2.at[0, k], r2.at[0, k]), (s2.at[1, k], r2.at[1, k]), r2_send, r2_recv, k)

    def joined(k):
        return both_ways((s3.at[0, k], r3.at[0, k]), (s3.at[1, k], r3.at[1, k]), r3_send, r3_recv, k)

    def give_back(k):
        return tuple(
            push(
                ret.at[k, j], back.at[k, pl.ds(pair * xh, pair)],
                back_send.at[j, k], back_recv.at[xh, k], (after, z_from(k) * 2 + j, t),
            )
            for j in range(2)
        )

    def given_back(k):
        return tuple(
            push(
                ret.at[k, j], back.at[k, pl.ds(pair * j, pair)],
                back_send.at[j, k], back_recv.at[j, k], to_right,
            )
            for j in range(2)
        )

    def ring_stage(k):
        @pl.when(k < nz - 1)
        def _():
            ring_in(k).wait_recv()

        @pl.when(k < nz - 3)
        def _():
            ring_next(k).start()

        for j in range(2):
            @pl.when(k == nz - 3 + j)
            def _(j=j):
                ring_last(j).start()

        @pl.when(k == nz - 1)
        def _():
            ring_last(0).wait_recv()
            ring_last(1).wait_recv()

    def partner_stage(k):
        slots_to_z(k).wait_recv()
        pick_for_partner(k)

    def gather_stage(k):
        push(xs.at[k], late_of(k, t), z_send.at[k], z_recv.at[k], to_right).wait_recv()
        start(gather(k))

    def forward_stage(k):
        arrive(gathered(k))
        start(forward(k, left, right))

    def up_stage(k):
        arrive(forward(k, opposite, opposite))
        over_x(k).wait_recv()
        chosen = picked(slot_in[k, pl.ds(xh, 1), :], (CAP * xh).astype(F32), pair)
        theirs = pl.ds(pl.multiple_of((MAIN + 2 * TAIL) * (1 - xh), 16), MAIN)
        middle = slice(MAIN, MAIN + 2 * TAIL)
        r, c = iota((2 * TAIL, 2 * TAIL), 0), iota((2 * TAIL, 2 * TAIL), 1)
        mine = (r < TAIL) == (xh == 1)
        for q in range(ny):
            xg[k, q, :, late:] = dot(chosen, xb[k, q]).astype(BF16)
            xg[k, q, theirs, late:] = pr[k, q * MAIN : (q + 1) * MAIN]
            shift = (mine & (c == r + TAIL * (q % 2) - TAIL * (1 - xh))).astype(BF16)
            first = packed_rows + (q // 2) * 2 * TAIL
            moved = dot(shift, pr[k, first : first + 2 * TAIL]).astype(BF16)
            xg[k, q, middle, late:] = xg[k, q, middle, late:] + moved
        acts = dot(xg[k, 0], wgu[:quarter, :])
        for q in range(1, ny):
            acts = acts + dot(xg[k, q], wgu[q * quarter : (q + 1) * quarter, :])
        gate_act, up_act = acts[:, :units], acts[:, units:]
        hidden[k] = (gate_act / (1.0 + jnp.exp(-gate_act)) * up_act).astype(BF16)
        part = dot(hidden[k], wd[opposite]).astype(BF16)
        s1[0, k] = part[:, :half]
        s1[1, k] = part[:, half:]
        start(relay(k))
        s2[0, k] = dot(hidden[k], wd[right, :, half:]).astype(BF16)
        s2[1, k] = dot(hidden[k], wd[left, :, :half]).astype(BF16)
        start(direct(k))

    def down_stage(k):
        arrive(relay(k))
        h = hidden[k]
        s3[0, k] = (dot(h, wd[right, :, :half]) + r1[0, k].astype(F32)).astype(BF16)
        s3[1, k] = (dot(h, wd[left, :, half:]) + r1[1, k].astype(F32)).astype(BF16)
        start(joined(k))

    def sum_stage(k):
        arrive(direct(k))
        arrive(joined(k))
        part = dot(hidden[k], wd[t])
        lo = part[:, :half] + r3[0, k].astype(F32) + r2[1, k].astype(F32)
        hi = part[:, half:] + r2[0, k].astype(F32) + r3[1, k].astype(F32)
        for j in range(2):
            first, tail = (MAIN + 2 * TAIL) * j, MAIN + TAIL * j
            ret[k, j, :MAIN] = lo[first : first + MAIN].astype(BF16)
            ret[k, j, MAIN : 2 * MAIN] = hi[first : first + MAIN].astype(BF16)
            tails = jnp.concatenate([lo[tail : tail + TAIL], hi[tail : tail + TAIL]], axis=0)
            ret[k, j, 2 * MAIN :] = tails.astype(BF16)
        start(give_back(k))

    def mix_stage(k):
        arrive(given_back(k))
        y = back[k]
        acc[:, :half] += dot(mix[k, 0, 0], y) + dot(mix[k, 0, 1], y)
        acc[:, half:] += dot(mix[k, 1, 0], y) + dot(mix[k, 1, 1], y)

    def leave(copies):
        for copy in copies:
            copy.wait_send()

    def drain_stage(k):
        @pl.when(k > 0)
        def _():
            leave((to_z(k), slots_to_z(k)))

        @pl.when((k > 0) & (k < nz - 3))
        def _():
            ring_next(k).wait_send()

        for copies in (
            gather(k), forward(k, left, right), relay(k), direct(k), joined(k), give_back(k),
        ):
            leave(copies)
        over_x(k).wait_send()

    def staged(i, lag, stage, first):
        p = i - lag

        @pl.when((p >= first) & (p < nz))
        def _():
            stage(chunk_at(p))

    def step(i, carry):
        staged(i, 2, sum_stage, 0)
        staged(i, 1, down_stage, 0)
        staged(i, -1, forward_stage, 0)

        def ring_and_partner():
            @pl.when(i < nz // 2)
            def _():
                ring_stage(2 * i + 1)

            @pl.when(i < nz // 2 - 1)
            def _():
                ring_stage(2 * i + 2)

            staged(i, -1, partner_stage, 1)

        pl.when(i > 0)(ring_and_partner)
        staged(i, 0, up_stage, 0)
        pl.when(i == 0)(ring_and_partner)
        staged(i, -2, gather_stage, 1)
        staged(i, -4, send_stage, 3)
        pl.when(i == 1)(turn_tables)
        staged(i, 2, weight_stage, 0)
        staged(i, 4, mix_stage, 0)
        staged(i, 5, drain_stage, 0)
        return carry

    lax.fori_loop(-1, nz + 5, step, 0)
    out_ref[...] = acc[...].astype(out_ref.dtype)

    leave((meta_x, meta_s, tok_x))
    leave(early_out())
    leave(early_pass(left, right))
    leave(ring_first())
    leave((ring_last(0), ring_last(1)))


def on_device(nsec, nz, ny, tokens, expert_ids, gate_values, w_gate, w_up, w_down):
    rows, quarter = tokens.shape[1:]
    width, units = w_gate.shape[2:]
    pair, half = 2 * CAP, quarter // 2
    late = 5 * quarter // 8
    early = quarter - late
    dma = pltpu.SemaphoreType.DMA
    vmem = lambda *shape, dtype=BF16: pltpu.VMEM(shape, dtype)
    sides = lambda n: [dma((2, n)), dma((2, n))]
    each = lambda n: [dma((n,)), dma((n,))]
    combined = pl.pallas_call(
        functools.partial(moe_kernel, nsec, nz, ny),
        out_shape=jax.ShapeDtypeStruct((rows, quarter), BF16),
        in_specs=[pl.BlockSpec(memory_space=pltpu.VMEM)] * 3 + [pl.BlockSpec(memory_space=pl.ANY)] * 3,
        out_specs=pl.BlockSpec(memory_space=pltpu.VMEM),
        scratch_shapes=[
            vmem(width, 2 * units), vmem(ny, units, quarter),
            vmem(3, NAMES, rows, dtype=F32),
            vmem(2, NAMES, rows, dtype=F32),
            vmem(2, rows, late),
            vmem(nz, pair, late),
            vmem(nz, ny, pair, quarter),
            vmem(nz, 8, rows, dtype=F32), vmem(nz, 8, rows, dtype=F32),
            vmem(nz, ny, rows, early),
            vmem(nz, ny * CAP, early), vmem(nz, ny * CAP, early),
            vmem(nz, pair, units),
            vmem(2, nz, pair, half), vmem(2, nz, pair, half),
            vmem(2, nz, pair, half), vmem(2, nz, pair, half),
            vmem(2, nz, pair, half), vmem(2, nz, pair, half),
            vmem(nz, 2, pair, half),
            vmem(nz, 2 * pair, half),
            vmem(2, rows, 128, dtype=F32),
            vmem(nz, 2, 2, rows, 2 * pair),
            vmem(rows, quarter, dtype=F32),
            dma((2 + ny,)), *each(2), dma, dma, *each(nz), *each(nz),
            *sides(1), *sides(1), *each(nz), *each(2), *each(nz),
            *sides(nz), *sides(nz), *sides(nz), *sides(nz), *sides(nz),
            *sides(nz),
        ],
        compiler_params=pltpu.CompilerParams(
            collective_id=0, has_side_effects=True, vmem_limit_bytes=60 * 1024 * 1024
        ),
        cost_estimate=pl.CostEstimate(
            flops=6 * nz * pair * width * units, bytes_accessed=6 * width * units, transcendentals=0
        ),
    )(tokens[0], expert_ids[0].T, gate_values[0].T, w_gate[0, 0], w_up[0, 0], w_down[0, 0])
    return combined[None]


def solution(mesh):
    nsec, nexp, ny = mesh.shape["section"], mesh.shape["expert"], mesh.shape["tensor"]
    in_specs = (
        P("section", "expert", "tensor"),
        P("section", "expert", None),
        P("section", "expert", None),
        P("section", "expert", None, "tensor"),
        P("section", "expert", None, "tensor"),
        P("section", "expert", "tensor", None),
    )
    return jax.shard_map(
        functools.partial(on_device, nsec, nexp // 2, ny),
        mesh=mesh, in_specs=in_specs, out_specs=P("section", "expert", "tensor"), check_vma=False,
    )
```
